512 devices in a mesh: dp: 32 (over z_lo, x), tensor: 16 (over y, z_hi, core).
Axes of the slice: x: 4, y: 4, z: 16 (z_hi: 2, z_lo: 8; z = z_hi * 8 + z_lo), core: 2. Of those that a mesh axis runs over, the one named last changes fastest.
Arguments:
- x_panel: bfloat16 [16384, 4096], P('dp', 'tensor'), may hold values from -6 to 6
- grad_hidden: bfloat16 [16384, 14336], P('dp', 'tensor'), may hold values from -0.046875 to 0.046875
- gate_blocks: bfloat16 [112, 8, 128, 128], P('tensor'), may hold values from -0.1875 to 0.1875
- up_blocks: bfloat16 [112, 8, 128, 128], P('tensor'), may hold values from -0.1875 to 0.1875
- block_rows: int32 [112, 8], P('tensor'), may hold values from 0 to 31, as said below
- block_owner: int32 [112, 8], P('tensor'), may hold values from 0 to 31, as said below
Outputs:
- grad_owned: float32 [16, 32, 2, 2, 128, 128], P('tensor', 'dp')
The draws below stay inside these ranges and needn't reach their ends.
Inputs may be any that keep to these rules, and one draw needn't show every extreme that they name: `block_rows`: the 8 block rows of one block column are distinct. `block_owner`: within each group of 7 consecutive block columns every dp index owns at most 2 blocks, and some index owns exactly 2.
All inputs are finite; a program needn't handle non-finite values.
Results may differ from the reference program's by a relative error of at most 0.013.
Values may be sent and summed in bfloat16 or wider, within the bound.
No kernel may reach another device: no remote copies, remote signals or barrier semaphores. Data moves between devices by JAX's collectives and lax.ppermute only.
A program may use at most 64 MiB of HBM per device.

```python
import jax
import jax.numpy as jnp
from jax import lax

D = 4096
FF = 14336
BS = 128
TOK_DEV = 512
KB = 8
COLS = 112
COLS_DEV = 7
TOKENS = 16384
OWNERS = 32
SHARDS = 16
CAP = 2


def draw_block_rows(key, part):
    key = jax.random.fold_in(key, 11)
    row_total = D // BS
    key_popular, key_jitter = jax.random.split(key)
    popular = jax.random.randint(key_popular, (1, row_total), 0, 4 * 65536)
    jitter = jax.random.randint(key_jitter, (COLS, row_total), 0, 65536)
    scores = (popular + jitter) * row_total + jnp.arange(row_total, dtype=jnp.int32)[None, :]
    chosen = lax.top_k(scores, KB)[1]
    return chosen.astype(jnp.int32)


def draw_block_owner(key, part):
    key = jax.random.fold_in(key, 23)
    block_count = COLS_DEV * KB
    slot_total = OWNERS * CAP

    def draw_shard(subkey):
        key_target, key_scores = jax.random.split(subkey)
        target_owner = jax.random.randint(key_target, (), 0, OWNERS)
        scores = jax.random.randint(key_scores, (slot_total,), 0, 1 << 20)
        owner_of = jnp.arange(slot_total, dtype=jnp.int32) // CAP
        scores = jnp.where(owner_of == target_owner, -1, scores)
        ranked = jnp.argsort(scores, stable=True)[:block_count]
        return (ranked // CAP).astype(jnp.int32)
    shard_keys = jax.random.split(key, COLS // COLS_DEV)
    owners = jax.vmap(draw_shard)(shard_keys)
    return owners.reshape(COLS, KB).astype(jnp.int32)


def steps_of(key, dims, shards, smallest, high):
    factor_of = 1.0
    for axis_at, parts in shards:
        draws = jax.random.uniform(jax.random.fold_in(jax.random.fold_in(key, 6), axis_at), (parts,), jnp.float32, smallest / len(shards), high / len(shards))
        factor_of = factor_of * jnp.repeat(jnp.exp(draws), dims[axis_at] // parts).reshape((-1,) + (1,) * (len(dims) - 1 - axis_at))
    return factor_of


def bell_draw(own_key, shape, spread, bound, cuts=(), held_as=jnp.bfloat16):
    array = jax.random.normal(own_key, shape, jnp.float32) * spread
    if len(cuts) > 0:
        array = steps_of(own_key, shape, cuts, -0.22, 0.18) * array
    return jnp.clip(array, min=-bound, max=bound).astype(held_as)


def setup_inputs(seed: int = 0) -> dict:
    keys = jax.random.split(jax.random.key(seed), 7)
    x_panel = bell_draw(keys[0], (TOKENS, D), 1.0, 6.0, ((0, 32), (1, 16)))
    grad_hidden = bell_draw(keys[1], (TOKENS, FF), TOKENS ** -0.5, 0.046875, ((0, 32), (1, 16)))
    gate_blocks = bell_draw(keys[2], (COLS, KB, BS, BS), (KB * BS) ** -0.5, 0.1875, ((0, 16),))
    up_blocks = bell_draw(keys[3], (COLS, KB, BS, BS), (KB * BS) ** -0.5, 0.1875, ((0, 16),))
    block_rows = draw_block_rows(jax.random.fold_in(keys[6], 71), 0)
    block_owner = draw_block_owner(jax.random.fold_in(keys[6], 71), 0)
    return dict(x_panel=x_panel, grad_hidden=grad_hidden, gate_blocks=gate_blocks, up_blocks=up_blocks, block_rows=block_rows, block_owner=block_owner)


def silu_parts(gate_pre):
    sigmoid_v = jax.nn.sigmoid(gate_pre)
    return gate_pre * sigmoid_v, sigmoid_v * (1.0 + gate_pre * (1.0 - sigmoid_v))


def reference(x_panel, grad_hidden, gate_blocks, up_blocks, block_rows, block_owner):
    token_count = x_panel.shape[0]
    row_blocks = x_panel.reshape(token_count, D // BS, BS)
    hidden_cols = jnp.transpose(grad_hidden.reshape(token_count, COLS, BS), (1, 0, 2))

    def column_work(operands):
        row_index, gate_w, up_w, grad_col = operands
        picked = row_blocks[:, row_index, :].reshape(token_count, KB * BS)
        gate_pre = jnp.dot(picked, gate_w.reshape(KB * BS, BS), preferred_element_type=jnp.float32)
        up_pre = jnp.dot(picked, up_w.reshape(KB * BS, BS), preferred_element_type=jnp.float32)
        activation, derivative = silu_parts(gate_pre)
        grad_f32 = grad_col.astype(jnp.float32)
        grad_gate_act = (grad_f32 * up_pre * derivative).astype(jnp.bfloat16)
        grad_up_act = (grad_f32 * activation).astype(jnp.bfloat16)
        paired = jnp.stack([grad_gate_act, grad_up_act], 1)
        panel_f32 = picked.astype(jnp.float32).reshape(OWNERS, TOK_DEV, KB, BS)
        paired_f32 = paired.astype(jnp.float32).reshape(OWNERS, TOK_DEV, 2, BS)
        partial_value = jnp.einsum('ntkb,ntme->nkmbe', panel_f32, paired_f32, precision=lax.Precision.HIGHEST)
        partial_value = partial_value.astype(jnp.bfloat16).astype(jnp.float32)
        return jnp.sum(partial_value, 0)

    grads = lax.map(column_work, (block_rows, gate_blocks, up_blocks, hidden_cols))
    block_count = COLS_DEV * KB
    owners = block_owner.reshape(SHARDS, block_count)
    onehot = (owners[:, :, None] == jnp.arange(OWNERS, dtype=jnp.int32)[None, None, :]).astype(jnp.int32)
    before = jnp.cumsum(onehot, 1) - onehot
    slot_index = jnp.sum(onehot * before, 2).astype(jnp.int32)
    shard_index = jnp.broadcast_to(jnp.arange(SHARDS, dtype=jnp.int32)[:, None], (SHARDS, block_count))
    grad_owned = jnp.zeros((SHARDS, OWNERS, CAP, 2, BS, BS), jnp.float32)
    grad_owned = grad_owned.at[shard_index, owners, slot_index].set(grads.reshape(SHARDS, block_count, 2, BS, BS))
    return grad_owned
```

```python
import functools

import jax
import jax.numpy as jnp
from jax import lax
from jax.experimental import pallas as pl
from jax.experimental.pallas import tpu as pltpu
from jax.sharding import Mesh, PartitionSpec as P

BS = 128
KB = 8
COLS = 7
BLOCKS = COLS * KB
TOK = 512
ROWS = 32
NX, NZ, CAP = 4, 8, 2
GROUP = NZ * CAP
AXES = {"zl": 8, "x": 4, "y": 4, "zh": 2, "core": 2}
VMEM = pl.BlockSpec(memory_space=pltpu.VMEM)
SMEM = pl.BlockSpec(memory_space=pltpu.SMEM)


def shift(value, axis, step):
    size = AXES[axis]
    return lax.ppermute(value, axis, [(i, (i + step) % size) for i in range(size)])


def flip(value, axis, bit):
    return lax.ppermute(value, axis, [(i, i ^ bit) for i in range(AXES[axis])])


def call(kernel, out_shape, in_specs, out_specs, scratch=(), flops=0, bytes_accessed=0):
    return pl.pallas_call(
        kernel,
        out_shape=out_shape,
        in_specs=in_specs,
        out_specs=out_specs,
        scratch_shapes=list(scratch),
        compiler_params=pltpu.CompilerParams(vmem_limit_bytes=40 * 1024 * 1024),
        cost_estimate=pl.CostEstimate(flops=flops, bytes_accessed=bytes_accessed, transcendentals=0),
    )


def table_kernel(owner_ref, table_ref, seen_ref):
    my_x = lax.axis_index("x")
    my_z = lax.axis_index("zl")

    def clear(i, carry):
        table_ref[i] = jnp.int32(-1)
        return carry

    lax.fori_loop(0, NX * GROUP, clear, 0)

    def clear_seen(i, carry):
        seen_ref[i] = jnp.int32(0)
        return carry

    lax.fori_loop(0, NX * NZ, clear_seen, 0)

    def place(i, carry):
        owner = owner_ref[i // KB, i % KB]
        slot = seen_ref[owner]
        seen_ref[owner] = slot + 1
        rel_x = (owner % NX - my_x + NX) % NX
        rel_z = (owner // NX) ^ my_z
        rel_z = (rel_z & 1) * 4 + (rel_z & 2) + (rel_z >> 2)
        table_ref[rel_x * GROUP + rel_z * CAP + slot] = i
        return carry

    lax.fori_loop(0, BLOCKS, place, 0)


def forward_kernel(a_ref, ac_ref, b_ref, bc_ref, w_ref, g_ref, rows_ref, x_ref, act_ref, picked_ref):
    zh = lax.axis_index("zh")
    core = lax.axis_index("core")
    for ref, z, c in ((a_ref, zh, core), (ac_ref, zh, 1 - core), (b_ref, 1 - zh, core), (bc_ref, 1 - zh, 1 - core)):
        for y in range(4):
            at = (y * 4 + z * 2 + c) * 2
            x_ref[at] = ref[y, :BS]
            x_ref[at + 1] = ref[y, BS:]

    def column(c, carry):
        for k in range(KB):
            picked_ref[k * BS:(k + 1) * BS] = x_ref[rows_ref[c, k]]
        pre = jnp.dot(w_ref[c], picked_ref[...], preferred_element_type=jnp.float32)
        gate, up = pre[:BS], pre[BS:]
        s = jax.nn.sigmoid(gate)
        h = g_ref[c].astype(jnp.float32)
        act_ref[c, :BS] = (h * up * (s * (1.0 + gate * (1.0 - s)))).astype(jnp.bfloat16)
        act_ref[c, BS:] = (h * (gate * s)).astype(jnp.bfloat16)
        return carry

    lax.fori_loop(0, COLS, column, 0)


def backward_kernel(group, dtype, x_ref, act_ref, rows_ref, table_ref, lo_ref, hi_ref):
    for i in range(GROUP):
        block = table_ref[group * GROUP + i]
        at = jnp.maximum(block, 0)
        c = at // KB
        value = lax.dot_general(
            x_ref[rows_ref[c, at % KB]], act_ref[c], (((1,), (1,)), ((), ())), preferred_element_type=jnp.float32
        )
        value = jnp.where(block >= 0, value, 0.0).astype(dtype)
        ref = lo_ref if i < GROUP // 2 else hi_ref
        row = (i % (GROUP // 2)) * 2 * BS
        ref[row:row + BS] = value[:, :BS]
        ref[row + BS:row + 2 * BS] = value[:, BS:]


def body(x_panel, grad_hidden, gate_blocks, up_blocks, block_rows, block_owner):
    bf16, f32 = jnp.bfloat16, jnp.float32
    table = call(
        table_kernel, jax.ShapeDtypeStruct((NX * GROUP,), jnp.int32), [SMEM], SMEM,
        [pltpu.SMEM((NX * NZ,), jnp.int32)],
    )(block_owner)
    own = x_panel.T
    far = flip(own, "zh", 1)
    weights = jnp.concatenate(
        [w.transpose(0, 3, 1, 2).reshape(COLS, BS, KB * BS) for w in (gate_blocks, up_blocks)], 1
    )
    hidden = grad_hidden.T.reshape(COLS, BS, TOK)
    a = lax.all_to_all(jnp.broadcast_to(own[None], (4,) + own.shape), "y", 0, 0, tiled=True)
    ac = flip(a, "core", 1)
    b = lax.all_to_all(jnp.broadcast_to(far[None], (4,) + far.shape), "y", 0, 0, tiled=True)
    bc = flip(b, "core", 1)

    x_all, act = call(
        forward_kernel,
        (jax.ShapeDtypeStruct((ROWS, BS, TOK), bf16), jax.ShapeDtypeStruct((COLS, 2 * BS, TOK), bf16)),
        [VMEM] * 6 + [SMEM], (VMEM, VMEM), [pltpu.VMEM((KB * BS, TOK), bf16)],
        flops=2 * COLS * KB * BS * 2 * BS * TOK, bytes_accessed=14 * 2**20,
    )(a, ac, b, bc, weights, hidden, block_rows)

    def backward(group, dtype):
        half = jax.ShapeDtypeStruct((GROUP * BS, BS), dtype)
        return call(
            functools.partial(backward_kernel, group, dtype), (half, half), [VMEM, VMEM, SMEM, SMEM], (VMEM, VMEM),
            flops=2 * GROUP * BS * 2 * BS * TOK, bytes_accessed=7 * 2**20,
        )(x_all, act, block_rows, table)

    p2a, p2b = backward(2, bf16)
    r2a = shift(p2a, "x", 1)
    r2b = shift(p2b, "x", -1)
    p1a, p1b = backward(1, bf16)
    r1b = shift(p1b, "x", 1)
    p3a, p3b = backward(3, bf16)
    r3a = shift(p3a, "x", -1)
    p0a, p0b = backward(0, f32)
    r1a = shift((p1a.astype(f32) + r2a.astype(f32)).astype(bf16), "x", 1)
    r3b = shift((p3b.astype(f32) + r2b.astype(f32)).astype(bf16), "x", -1)
    send = (p0b + r1b.astype(f32) + r3b.astype(f32)).astype(bf16)
    got = flip(send, "zl", 1)
    keep = p0a + r1a.astype(f32) + r3a.astype(f32) + got.astype(f32)
    half = keep.shape[0] // 2
    got = flip(keep[half:].astype(bf16), "zl", 2)
    keep = keep[:half] + got.astype(f32)
    half = half // 2
    got = flip(keep[half:].astype(bf16), "zl", 4)
    keep = keep[:half] + got.astype(f32)
    return keep.reshape(1, 1, CAP, 2, BS, BS)


def solution(mesh):
    fine = Mesh(mesh.devices.reshape(tuple(AXES.values())), tuple(AXES))
    dp, tensor = ("zl", "x"), ("y", "zh", "core")
    in_specs = (
        P(dp, tensor),
        P(dp, tensor),
        P(tensor, None, None, None),
        P(tensor, None, None, None),
        P(tensor, None),
        P(tensor, None),
    )
    out_specs = P(tensor, dp, None, None, None, None)
    return jax.shard_map(body, mesh=fine, in_specs=in_specs, out_specs=out_specs, check_vma=False)
```

```python
import functools

import jax
import jax.numpy as jnp
from jax import lax
from jax.experimental import pallas as pl
from jax.experimental.pallas import tpu as pltpu
from jax.sharding import Mesh, PartitionSpec as P

BS = 128
KB = 8
COLS = 7
BLOCKS = COLS * KB
TOK = 512
ROWS = 32
NX, NZ, CAP = 4, 8, 2
GROUP = NZ * CAP
AXES = {"zl": 8, "x": 4, "y": 4, "zh": 2, "core": 2}
VMEM = pl.BlockSpec(memory_space=pltpu.VMEM)
SMEM = pl.BlockSpec(memory_space=pltpu.SMEM)


def shift(value, axis, step):
    size = AXES[axis]
    return lax.ppermute(value, axis, [(i, (i + step) % size) for i in range(size)])


def climb(value, step):
    perm = []
    for z in range(16):
        to = (z + step) % 16
        perm.append((z % 8 * 2 + z // 8, to % 8 * 2 + to // 8))
    return lax.ppermute(value, ("zl", "zh"), perm)


def flip(value, axis, bit):
    return lax.ppermute(value, axis, [(i, i ^ bit) for i in range(AXES[axis])])


def call(kernel, out_shape, in_specs, out_specs, scratch=(), flops=0, bytes_accessed=0):
    return pl.pallas_call(
        kernel,
        out_shape=out_shape,
        in_specs=in_specs,
        out_specs=out_specs,
        scratch_shapes=list(scratch),
        compiler_params=pltpu.CompilerParams(vmem_limit_bytes=8 * 1024 * 1024),
        cost_estimate=pl.CostEstimate(flops=flops, bytes_accessed=bytes_accessed, transcendentals=0),
    )


def table_kernel(owner_ref, table_ref, seen_ref):
    my_x = lax.axis_index("x")
    my_z = lax.axis_index("zl")

    def clear(i, carry):
        table_ref[i] = jnp.int32(-1)
        return carry

    lax.fori_loop(0, NX * GROUP, clear, 0)

    def clear_seen(i, carry):
        seen_ref[i] = jnp.int32(0)
        return carry

    lax.fori_loop(0, NX * NZ, clear_seen, 0)

    def place(i, carry):
        owner = owner_ref[i // KB, i % KB]
        slot = seen_ref[owner]
        seen_ref[owner] = slot + 1
        rel_x = (owner % NX - my_x + NX) % NX
        rel_z = (owner // NX) ^ my_z
        rel_z = (rel_z & 1) * 4 + (rel_z & 2) + (rel_z >> 2)
        table_ref[rel_x * GROUP + rel_z * CAP + slot] = i
        return carry

    lax.fori_loop(0, BLOCKS, place, 0)


def forward_kernel(a_ref, ac_ref, b_ref, bc_ref, w_ref, g_ref, rows_ref, x_ref, act_ref, picked_ref):
    zh = lax.axis_index("zh")
    core = lax.axis_index("core")
    for ref, z, c in ((a_ref, zh, core), (ac_ref, zh, 1 - core), (b_ref, 1 - zh, core), (bc_ref, 1 - zh, 1 - core)):
        for y in range(4):
            at = (y * 4 + z * 2 + c) * 2
            x_ref[at] = ref[y, :BS]
            x_ref[at + 1] = ref[y, BS:]

    def column(c, carry):
        for k in range(KB):
            picked_ref[k * BS:(k + 1) * BS] = x_ref[rows_ref[c, k]]
        pre = jnp.dot(w_ref[c], picked_ref[...], preferred_element_type=jnp.float32)
        gate, up = pre[:BS], pre[BS:]
        s = jax.nn.sigmoid(gate)
        h = g_ref[c].astype(jnp.float32)
        act_ref[c, :BS] = (h * up * (s * (1.0 + gate * (1.0 - s)))).astype(jnp.bfloat16)
        act_ref[c, BS:] = (h * (gate * s)).astype(jnp.bfloat16)
        return carry

    lax.fori_loop(0, COLS, column, 0, unroll=True)


def backward_kernel(group, dtype, x_ref, act_ref, rows_ref, table_ref, lo_ref, hi_ref):
    for i in range(GROUP):
        block = table_ref[group * GROUP + i]
        at = jnp.maximum(block, 0)
        c = at // KB
        value = lax.dot_general(
            x_ref[rows_ref[c, at % KB]], act_ref[c], (((1,), (1,)), ((), ())), preferred_element_type=jnp.float32
        )
        value = jnp.where(block >= 0, value, 0.0).astype(dtype)
        ref = lo_ref if i < GROUP // 2 else hi_ref
        row = (i % (GROUP // 2)) * 2 * BS
        ref[row:row + BS] = value[:, :BS]
        ref[row + BS:row + 2 * BS] = value[:, BS:]


def body(x_panel, grad_hidden, gate_blocks, up_blocks, block_rows, block_owner):
    bf16, f32 = jnp.bfloat16, jnp.float32
    table = call(
        table_kernel, jax.ShapeDtypeStruct((NX * GROUP,), jnp.int32), [SMEM], SMEM,
        [pltpu.SMEM((NX * NZ,), jnp.int32)],
    )(block_owner)
    own = x_panel.T
    up, down = climb(own[:BS], 4), climb(own[BS:], -4)
    a = lax.all_to_all(jnp.broadcast_to(own[None], (4,) + own.shape), "y", 0, 0, tiled=True)
    ac = flip(a, "core", 1)
    gate_t, up_t = (w.transpose(0, 3, 1, 2).reshape(COLS, BS, KB * BS) for w in (gate_blocks, up_blocks))
    up, down, gate_t = lax.optimization_barrier((up, down, gate_t))
    up, down = climb(up, 4), climb(down, -4)
    weights = jnp.concatenate([gate_t, up_t], 1)
    hidden = grad_hidden.T.reshape(COLS, BS, TOK)
    up, down, weights, hidden, table = lax.optimization_barrier((up, down, weights, hidden, table))
    far = jnp.concatenate([up, down], 0)
    b = lax.all_to_all(jnp.broadcast_to(far[None], (4,) + far.shape), "y", 0, 0, tiled=True)
    bc = flip(b, "core", 1)

    x_all, act = call(
        forward_kernel,
        (jax.ShapeDtypeStruct((ROWS, BS, TOK), bf16), jax.ShapeDtypeStruct((COLS, 2 * BS, TOK), bf16)),
        [VMEM] * 6 + [SMEM], (VMEM, VMEM), [pltpu.VMEM((KB * BS, TOK), bf16)],
        flops=2 * COLS * KB * BS * 2 * BS * TOK, bytes_accessed=14 * 2**20,
    )(a, ac, b, bc, weights, hidden, block_rows)

    def backward(group, dtype):
        half = jax.ShapeDtypeStruct((GROUP * BS, BS), dtype)
        return call(
            functools.partial(backward_kernel, group, dtype), (half, half), [VMEM, VMEM, SMEM, SMEM], (VMEM, VMEM),
            flops=2 * GROUP * BS * 2 * BS * TOK, bytes_accessed=7 * 2**20,
        )(x_all, act, block_rows, table)

    p2a, p2b = backward(2, bf16)
    r2a = shift(p2a, "x", 1)
    r2b = shift(p2b, "x", -1)
    p1a, p1b = backward(1, bf16)
    r1b = shift(p1b, "x", 1)
    p3a, p3b = backward(3, bf16)
    r3a = shift(p3a, "x", -1)
    p0a, p0b = backward(0, f32)
    r1a = shift((p1a.astype(f32) + r2a.astype(f32)).astype(bf16), "x", 1)
    r3b = shift((p3b.astype(f32) + r2b.astype(f32)).astype(bf16), "x", -1)
    send = (p0b + r1b.astype(f32) + r3b.astype(f32)).astype(bf16)
    got = flip(send, "zl", 1)
    keep = p0a + r1a.astype(f32) + r3a.astype(f32) + got.astype(f32)
    half = keep.shape[0] // 2
    got = flip(keep[half:].astype(bf16), "zl", 2)
    keep = keep[:half] + got.astype(f32)
    half = half // 2
    got = flip(keep[half:].astype(bf16), "zl", 4)
    keep = keep[:half] + got.astype(f32)
    return keep.reshape(1, 1, CAP, 2, BS, BS)


def solution(mesh):
    fine = Mesh(mesh.devices.reshape(tuple(AXES.values())), tuple(AXES))
    dp, tensor = ("zl", "x"), ("y", "zh", "core")
    in_specs = (
        P(dp, tensor),
        P(dp, tensor),
        P(tensor, None, None, None),
        P(tensor, None, None, None),
        P(tensor, None),
        P(tensor, None),
    )
    out_specs = P(tensor, dp, None, None, None, None)
    return jax.shard_map(body, mesh=fine, in_specs=in_specs, out_specs=out_specs, check_vma=False)
```

```python
import functools

import jax
import jax.numpy as jnp
from jax import lax
from jax.experimental import pallas as pl
from jax.experimental.pallas import tpu as pltpu
from jax.sharding import Mesh, PartitionSpec as P

BS = 128
KB = 8
COLS = 7
BLOCKS = COLS * KB
TOK = 512
ROWS = 32
NX, NZ, CAP = 4, 8, 2
AXES = {"zl": 8, "x": 4, "y": 4, "zh": 2, "core": 2}
VMEM = pl.BlockSpec(memory_space=pltpu.VMEM)
SMEM = pl.BlockSpec(memory_space=pltpu.SMEM)


def climb(value, step):
    perm = []
    for z in range(16):
        to = (z + step) % 16
        perm.append((z % 8 * 2 + z // 8, to % 8 * 2 + to // 8))
    return lax.ppermute(value, ("zl", "zh"), perm)


def flip(value, axis, bit):
    return lax.ppermute(value, axis, [(i, i ^ bit) for i in range(AXES[axis])])


def call(kernel, out_shape, in_specs, out_specs, scratch=(), flops=0, bytes_accessed=0):
    return pl.pallas_call(
        kernel,
        out_shape=out_shape,
        in_specs=in_specs,
        out_specs=out_specs,
        scratch_shapes=list(scratch),
        compiler_params=pltpu.CompilerParams(vmem_limit_bytes=8 * 1024 * 1024),
        cost_estimate=pl.CostEstimate(flops=flops, bytes_accessed=bytes_accessed, transcendentals=0),
    )


def table_kernel(owner_ref, table_ref, seen_ref):
    my_z = lax.axis_index("zl")

    def clear(i, carry):
        table_ref[i] = jnp.int32(-1)
        return carry

    lax.fori_loop(0, NX * NZ * CAP, clear, 0)

    def clear_seen(i, carry):
        seen_ref[i] = jnp.int32(0)
        return carry

    lax.fori_loop(0, NX * NZ, clear_seen, 0)

    def place(i, carry):
        owner = owner_ref[i // KB, i % KB]
        slot = seen_ref[owner]
        seen_ref[owner] = slot + 1
        x = owner % NX
        rel_z = (owner // NX) ^ my_z
        odd = rel_z & 1
        rest = (rel_z & 2) + (rel_z >> 2)
        first = x * NZ + odd * 4 + rest
        second = NX * NZ + (1 - odd) * (NX * 4) + x * 4 + rest
        table_ref[jnp.where(slot == 0, first, second)] = i
        return carry

    lax.fori_loop(0, BLOCKS, place, 0)


def forward_kernel(a_ref, ac_ref, b_ref, bc_ref, gate_ref, up_ref, g_ref, rows_ref, x_ref, act_ref, picked_ref):
    zh = lax.axis_index("zh")
    core = lax.axis_index("core")
    for ref, z, c in ((a_ref, zh, core), (ac_ref, zh, 1 - core), (b_ref, 1 - zh, core), (bc_ref, 1 - zh, 1 - core)):
        for y in range(4):
            at = (y * 4 + z * 2 + c) * 2
            x_ref[at] = ref[y, :BS]
            x_ref[at + 1] = ref[y, BS:]

    def column(c, carry):
        for k in range(KB):
            picked_ref[k * BS:(k + 1) * BS] = x_ref[rows_ref[c, k]]
        weights = jnp.concatenate([gate_ref[c], up_ref[c]], 0)
        pre = jnp.dot(weights, picked_ref[...], preferred_element_type=jnp.float32)
        gate, up = pre[:BS], pre[BS:]
        s = jax.nn.sigmoid(gate)
        h = g_ref[c].astype(jnp.float32)
        act_ref[c, :BS] = (h * up * (s * (1.0 + gate * (1.0 - s)))).astype(jnp.bfloat16)
        act_ref[c, BS:] = (h * (gate * s)).astype(jnp.bfloat16)
        return carry

    lax.fori_loop(0, COLS, column, 0, unroll=True)


def backward_kernel(first, count, dtype, x_ref, act_ref, rows_ref, table_ref, out_ref):
    for i in range(count):
        block = table_ref[first + i]
        at = jnp.maximum(block, 0)
        c = at // KB
        value = lax.dot_general(
            x_ref[rows_ref[c, at % KB]], act_ref[c], (((1,), (1,)), ((), ())), preferred_element_type=jnp.float32
        )
        value = jnp.where(block >= 0, value, 0.0).astype(dtype)
        out_ref[2 * i * BS:(2 * i + 1) * BS] = value[:, :BS]
        out_ref[(2 * i + 1) * BS:(2 * i + 2) * BS] = value[:, BS:]


def body(x_panel, grad_hidden, gate_blocks, up_blocks, block_rows, block_owner):
    bf16, f32 = jnp.bfloat16, jnp.float32
    table = call(
        table_kernel, jax.ShapeDtypeStruct((NX * NZ * CAP,), jnp.int32), [SMEM], SMEM,
        [pltpu.SMEM((NX * NZ,), jnp.int32)],
    )(block_owner)
    own = x_panel.T
    up, down = climb(own[:BS], 4), climb(own[BS:], -4)
    gate_t, up_t = (w.transpose(0, 3, 1, 2).reshape(COLS, BS, KB * BS) for w in (gate_blocks, up_blocks))
    hidden = grad_hidden.T.reshape(COLS, BS, TOK)
    own, gate_t = lax.optimization_barrier((own, gate_t))
    a = lax.all_to_all(jnp.broadcast_to(own[None], (4,) + own.shape), "y", 0, 0, tiled=True)
    ac = flip(a, "core", 1)
    up, down = climb(up, 4), climb(down, -4)
    up, down, up_t, hidden = lax.optimization_barrier((up, down, up_t, hidden))
    far = jnp.concatenate([up, down], 0)
    b = lax.all_to_all(jnp.broadcast_to(far[None], (4,) + far.shape), "y", 0, 0, tiled=True)
    b, table = lax.optimization_barrier((b, table))
    bc = flip(b, "core", 1)

    x_all, act = call(
        forward_kernel,
        (jax.ShapeDtypeStruct((ROWS, BS, TOK), bf16), jax.ShapeDtypeStruct((COLS, 2 * BS, TOK), bf16)),
        [VMEM] * 7 + [SMEM], (VMEM, VMEM), [pltpu.VMEM((KB * BS, TOK), bf16)],
        flops=2 * COLS * KB * BS * 2 * BS * TOK, bytes_accessed=14 * 2**20,
    )(a, ac, b, bc, gate_t, up_t, hidden, block_rows)

    def backward(first, count, dtype):
        return call(
            functools.partial(backward_kernel, first, count, dtype),
            jax.ShapeDtypeStruct((count * 2 * BS, BS), dtype), [VMEM, VMEM, SMEM, SMEM], VMEM,
            flops=2 * count * BS * 2 * BS * TOK, bytes_accessed=7 * 2**20,
        )(x_all, act, block_rows, table)

    def over_x(value):
        value = value.reshape(NX, value.shape[0] // NX, BS)
        return lax.all_to_all(value, "x", 0, 0, tiled=True)

    def halve(keep, bit):
        half = keep.shape[0] // 2
        got = flip(keep[half:].astype(bf16), "zl", bit)
        return keep[:half] + got.astype(f32)

    got = flip(backward(NX * NZ, NX * 4, bf16), "zl", 1)
    first = over_x(backward(0, NX * NZ, bf16))
    second = (backward(NX * NZ + NX * 4, NX * 4, f32) + got.astype(f32)).astype(bf16)
    first, second = lax.optimization_barrier((first, second))
    second = over_x(second)
    half = first.shape[1] // 2
    got = flip(jnp.sum(first[:, half:].astype(f32), 0).astype(bf16), "zl", 1)
    first = jnp.sum(first[:, :half].astype(f32), 0) + got.astype(f32)
    first = halve(halve(first, 2), 4)
    second = halve(halve(jnp.sum(second.astype(f32), 0), 2), 4)
    return jnp.concatenate([first, second], 0).reshape(1, 1, CAP, 2, BS, BS)


def solution(mesh):
    fine = Mesh(mesh.devices.reshape(tuple(AXES.values())), tuple(AXES))
    dp, tensor = ("zl", "x"), ("y", "zh", "core")
    in_specs = (
        P(dp, tensor),
        P(dp, tensor),
        P(tensor, None, None, None),
        P(tensor, None, None, None),
        P(tensor, None),
        P(tensor, None),
    )
    out_specs = P(tensor, dp, None, None, None, None)
    return jax.shard_map(body, mesh=fine, in_specs=in_specs, out_specs=out_specs, check_vma=False)
```

```python
import functools

import jax
import jax.numpy as jnp
from jax import lax
from jax.experimental import pallas as pl
from jax.experimental.pallas import tpu as pltpu
from jax.sharding import Mesh, PartitionSpec as P

BS = 128
KB = 8
COLS = 7
BLOCKS = COLS * KB
TOK = 512
ROWS = 32
NX, NZ, CAP = 4, 8, 2
AXES = {"zl": 8, "x": 4, "y": 4, "zh": 2, "core": 2}
Y_STEPS = (0, 1, -1, 2)
VMEM = pl.BlockSpec(memory_space=pltpu.VMEM)
ANY = pl.BlockSpec(memory_space=pl.ANY)
SMEM = pl.BlockSpec(memory_space=pltpu.SMEM)


def shift(value, axis, step):
    size = AXES[axis]
    return lax.ppermute(value, axis, [(i, (i + step) % size) for i in range(size)])


def flip(value, axis, bit):
    return lax.ppermute(value, axis, [(i, i ^ bit) for i in range(AXES[axis])])


def call(kernel, out_shape, in_specs, out_specs, scratch=(), flops=0, bytes_accessed=0):
    return pl.pallas_call(
        kernel,
        out_shape=out_shape,
        in_specs=in_specs,
        out_specs=out_specs,
        scratch_shapes=list(scratch),
        compiler_params=pltpu.CompilerParams(vmem_limit_bytes=8 * 1024 * 1024),
        cost_estimate=pl.CostEstimate(flops=flops, bytes_accessed=bytes_accessed, transcendentals=0),
    )


def table_kernel(owner_ref, gate_ref, up_ref, hidden_ref, table_ref, seen_ref):
    my_z = lax.axis_index("zl")

    def clear(i, carry):
        table_ref[i] = jnp.int32(-1)
        return carry

    lax.fori_loop(0, NX * NZ * CAP, clear, 0)

    def clear_seen(i, carry):
        seen_ref[i] = jnp.int32(0)
        return carry

    lax.fori_loop(0, NX * NZ, clear_seen, 0)

    def place(i, carry):
        owner = owner_ref[i // KB, i % KB]
        slot = seen_ref[owner]
        seen_ref[owner] = slot + 1
        x = owner % NX
        rel_z = (owner // NX) ^ my_z
        odd = rel_z & 1
        rest = (rel_z & 2) + (rel_z >> 2)
        first = x * NZ + odd * 4 + rest
        second = NX * NZ + (1 - odd) * (NX * 4) + x * 4 + rest
        table_ref[jnp.where(slot == 0, first, second)] = i
        return carry

    lax.fori_loop(0, BLOCKS, place, 0)


def forward_kernel(a_ref, ac_ref, b_ref, bc_ref, gate_ref, up_ref, g_ref, rows_ref, x_ref, act_ref, picked_ref):
    zh = lax.axis_index("zh")
    core = lax.axis_index("core")
    me = lax.axis_index("y")
    for c, near_ref, far_ref in ((core, a_ref, b_ref), (1 - core, ac_ref, bc_ref)):
        for i, step in enumerate(Y_STEPS):
            at = ((me - step + 4) % 4 * 4 + zh * 2 + c) * 2
            x_ref[at] = near_ref[i, :BS]
            x_ref[at + 1] = near_ref[i, BS:]
            at = (i * 4 + (1 - zh) * 2 + c) * 2
            x_ref[at] = far_ref[i, :BS]
            x_ref[at + 1] = far_ref[i, BS:]

    def column(c, carry):
        for k in range(KB):
            picked_ref[k * BS:(k + 1) * BS] = x_ref[rows_ref[c, k]]
        weights = jnp.concatenate([gate_ref[c], up_ref[c]], 0)
        pre = jnp.dot(weights, picked_ref[...], preferred_element_type=jnp.float32)
        gate, up = pre[:BS], pre[BS:]
        s = jax.nn.sigmoid(gate)
        h = g_ref[c].astype(jnp.float32)
        act_ref[c, :BS] = (h * up * (s * (1.0 + gate * (1.0 - s)))).astype(jnp.bfloat16)
        act_ref[c, BS:] = (h * (gate * s)).astype(jnp.bfloat16)
        return carry

    lax.fori_loop(0, COLS, column, 0, unroll=True)


def backward_kernel(first, count, dtype, x_ref, act_ref, rows_ref, table_ref, out_ref):
    for i in range(count):
        block = table_ref[first + i]
        at = jnp.maximum(block, 0)
        c = at // KB
        value = lax.dot_general(
            x_ref[rows_ref[c, at % KB]], act_ref[c], (((1,), (1,)), ((), ())), preferred_element_type=jnp.float32
        )
        value = jnp.where(block >= 0, value, 0.0).astype(dtype)
        out_ref[2 * i * BS:(2 * i + 1) * BS] = value[:, :BS]
        out_ref[(2 * i + 1) * BS:(2 * i + 2) * BS] = value[:, BS:]


def sum_kernel(got_ref, order_ref, send_ref, keep_ref):
    half = got_ref.shape[1] // 2
    for ref, at in ((keep_ref, 0), (send_ref, half)):
        rows = slice(at, at + half)
        total = got_ref[0, rows].astype(jnp.float32)
        for i in range(1, NX):
            total += got_ref[i, rows].astype(jnp.float32)
        ref[...] = total.astype(ref.dtype)


def body(x_panel, grad_hidden, gate_blocks, up_blocks, block_rows, block_owner):
    bf16, f32 = jnp.bfloat16, jnp.float32
    own = x_panel.T
    far = flip(own, "zh", 1)
    gate_t, up_t = (w.transpose(0, 3, 1, 2).reshape(COLS, BS, KB * BS) for w in (gate_blocks, up_blocks))
    hidden = grad_hidden.T.reshape(COLS, BS, TOK)
    a = jnp.stack([own] + [shift(own, "y", step) for step in Y_STEPS[1:]])
    ac = flip(a, "core", 1)
    corners = [v[0, :8] for v in (gate_t, up_t, hidden)]
    table = call(
        table_kernel, jax.ShapeDtypeStruct((NX * NZ * CAP,), jnp.int32), [SMEM] + [ANY] * 3, SMEM,
        [pltpu.SMEM((NX * NZ,), jnp.int32)],
    )(block_owner, *corners)
    far, table = lax.optimization_barrier((far, table))
    b = lax.all_to_all(jnp.broadcast_to(far[None], (4,) + far.shape), "y", 0, 0, tiled=True)
    bc = flip(b, "core", 1)

    x_all, act = call(
        forward_kernel,
        (jax.ShapeDtypeStruct((ROWS, BS, TOK), bf16), jax.ShapeDtypeStruct((COLS, 2 * BS, TOK), bf16)),
        [VMEM] * 7 + [SMEM], (VMEM, VMEM), [pltpu.VMEM((KB * BS, TOK), bf16)],
        flops=2 * COLS * KB * BS * 2 * BS * TOK, bytes_accessed=14 * 2**20,
    )(a, ac, b, bc, gate_t, up_t, hidden, block_rows)

    def backward(first, count, dtype):
        return call(
            functools.partial(backward_kernel, first, count, dtype),
            jax.ShapeDtypeStruct((count * 2 * BS, BS), dtype), [VMEM, VMEM, SMEM, SMEM], VMEM,
            flops=2 * count * BS * 2 * BS * TOK, bytes_accessed=7 * 2**20,
        )(x_all, act, block_rows, table)

    def over_x(value):
        value = value.reshape(NX, value.shape[0] // NX, BS)
        return lax.all_to_all(value, "x", 0, 0, tiled=True)

    got = flip(backward(NX * NZ, NX * 4, bf16), "zl", 1)
    first = over_x(backward(0, NX * NZ, bf16))
    second = (backward(NX * NZ + NX * 4, NX * 4, f32) + got.astype(f32)).astype(bf16)
    half = first.shape[1] // 2
    send, first = call(
        sum_kernel, (jax.ShapeDtypeStruct((half, BS), bf16), jax.ShapeDtypeStruct((half, BS), f32)),
        [VMEM, ANY], (VMEM, VMEM), bytes_accessed=3 * 2**20,
    )(first, second)
    second = over_x(second)
    first = first + flip(send, "zl", 1).astype(f32)
    both = [first, jnp.sum(second.astype(f32), 0)]
    for bit in (2, 4):
        half = half // 2
        got = flip(jnp.concatenate([v[half:].astype(bf16) for v in both], 0), "zl", bit)
        both = [v[:half] + got[i * half:(i + 1) * half].astype(f32) for i, v in enumerate(both)]
    return jnp.concatenate(both, 0).reshape(1, 1, CAP, 2, BS, BS)


def solution(mesh):
    fine = Mesh(mesh.devices.reshape(tuple(AXES.values())), tuple(AXES))
    dp, tensor = ("zl", "x"), ("y", "zh", "core")
    in_specs = (
        P(dp, tensor),
        P(dp, tensor),
        P(tensor, None, None, None),
        P(tensor, None, None, None),
        P(tensor, None),
        P(tensor, None),
    )
    out_specs = P(tensor, dp, None, None, None, None)
    return jax.shard_map(body, mesh=fine, in_specs=in_specs, out_specs=out_specs, check_vma=False)
```

```python
import functools

import jax
import jax.numpy as jnp
from jax import lax
from jax.experimental import pallas as pl
from jax.experimental.pallas import tpu as pltpu
from jax.sharding import Mesh, PartitionSpec as P

BS = 128
KB = 8
COLS = 7
BLOCKS = COLS * KB
TOK = 512
ROWS = 32
NX, NZ, CAP = 4, 8, 2
AXES = {"z4": 4, "z2": 2, "x": 4, "y": 4, "zh": 2, "core": 2}
VMEM = pl.BlockSpec(memory_space=pltpu.VMEM)
ANY = pl.BlockSpec(memory_space=pl.ANY)
SMEM = pl.BlockSpec(memory_space=pltpu.SMEM)


def swap(value, axis):
    return lax.ppermute(value, axis, [(0, 1), (1, 0)])


def spread(value, axis):
    return lax.all_to_all(jnp.broadcast_to(value[None], (AXES[axis],) + value.shape), axis, 0, 0, tiled=True)


def call(kernel, out_shape, in_specs, out_specs, scratch=(), flops=0, bytes_accessed=0):
    return pl.pallas_call(
        kernel,
        out_shape=out_shape,
        in_specs=in_specs,
        out_specs=out_specs,
        scratch_shapes=list(scratch),
        compiler_params=pltpu.CompilerParams(vmem_limit_bytes=40 * 1024 * 1024),
        cost_estimate=pl.CostEstimate(flops=flops, bytes_accessed=bytes_accessed, transcendentals=0),
    )


def place_kernel(owner_ref, gate_ref, up_ref, hidden_ref, near_ref, place_ref, seen_ref):
    my_z = lax.axis_index("z2")

    def clear(i, carry):
        seen_ref[i] = jnp.int32(0)
        return carry

    lax.fori_loop(0, NX * NZ, clear, 0)

    def place(i, carry):
        owner = owner_ref[i // KB, i % KB]
        slot = seen_ref[owner]
        seen_ref[owner] = slot + 1
        x = owner % NX
        z = owner // NX
        other = (z & 1) ^ my_z
        first = x * NZ + other * 4 + (z >> 1)
        second = NX * NZ + (1 - other) * (NX * 4) + x * 4 + (z >> 1)
        place_ref[i] = jnp.where(slot == 0, first, second)
        return carry

    lax.fori_loop(0, BLOCKS, place, 0)


def block_kernel(
    a_ref, ac_ref, b_ref, bc_ref, gate_ref, up_ref, hidden_ref, rows_ref, place_ref,
    first_ref, send_ref, keep_ref, x_ref, w_ref, h_ref, picked_ref, out_ref, x_sem, w_sem, out_sem,
):
    zh = lax.axis_index("zh")
    core = lax.axis_index("core")
    x_copies = []
    for i, (ref, z, c) in enumerate(
        ((a_ref, zh, core), (ac_ref, zh, 1 - core), (b_ref, 1 - zh, core), (bc_ref, 1 - zh, 1 - core))
    ):
        for y in range(4):
            at = (y * 4 + z * 2 + c) * 2
            x_copies.append(pltpu.make_async_copy(ref.at[y], x_ref.at[pl.ds(at, 2)], x_sem.at[i * 4 + y]))
    w_copies = []
    for c in range(COLS):
        w_copies.append((
            pltpu.make_async_copy(gate_ref.at[c], w_ref.at[c, pl.ds(0, BS)], w_sem.at[3 * c]),
            pltpu.make_async_copy(up_ref.at[c], w_ref.at[c, pl.ds(BS, BS)], w_sem.at[3 * c + 1]),
            pltpu.make_async_copy(hidden_ref.at[c], h_ref.at[c], w_sem.at[3 * c + 2]),
        ))
    for copy in x_copies:
        copy.start()
    for copies in w_copies:
        for copy in copies:
            copy.start()
    out_ref[...] = jnp.zeros_like(out_ref)
    for copy in x_copies:
        copy.wait()
    for c in range(COLS):
        for k in range(KB):
            picked_ref[k * BS:(k + 1) * BS] = x_ref[rows_ref[c, k]]
        for copy in w_copies[c]:
            copy.wait()
        picked = picked_ref[...]
        pre = jnp.dot(w_ref[c], picked, preferred_element_type=jnp.float32)
        gate, up = pre[:BS], pre[BS:]
        s = jax.nn.sigmoid(gate)
        h = h_ref[c].astype(jnp.float32)
        grad_gate = (h * up * (s * (1.0 + gate * (1.0 - s)))).astype(jnp.bfloat16)
        grad_up = (h * (gate * s)).astype(jnp.bfloat16)
        for m, act in enumerate((grad_gate, grad_up)):
            value = lax.dot_general(
                picked, act, (((1,), (1,)), ((), ())), preferred_element_type=jnp.float32
            ).astype(jnp.bfloat16)
            for k in range(KB):
                out_ref[place_ref[c * KB + k], m * BS:(m + 1) * BS] = value[k * BS:(k + 1) * BS]
    out_copies = []
    at = 0
    for i, ref in enumerate((send_ref, first_ref, keep_ref)):
        at = (NX * NZ, 0, NX * NZ + NX * 4)[i]
        out_copies.append(pltpu.make_async_copy(out_ref.at[pl.ds(at, ref.shape[0])], ref, out_sem.at[i]))
    for copy in out_copies:
        copy.start()
    for copy in out_copies:
        copy.wait()


def sum_kernel(got_ref, order_ref, send_ref, keep_ref):
    half = got_ref.shape[1] // 2
    for ref, at in ((keep_ref, 0), (send_ref, half)):
        rows = slice(at, at + half)
        total = got_ref[0, rows].astype(jnp.float32)
        for i in range(1, NX):
            total += got_ref[i, rows].astype(jnp.float32)
        ref[...] = total.astype(ref.dtype)


def body(x_panel, grad_hidden, gate_blocks, up_blocks, block_rows, block_owner):
    bf16, f32 = jnp.bfloat16, jnp.float32
    own = x_panel.T.reshape(2, BS, TOK)
    far = swap(own, "zh")
    a = spread(own, "y")
    gate_t, up_t = (w.transpose(0, 3, 1, 2).reshape(COLS, BS, KB * BS) for w in (gate_blocks, up_blocks))
    hidden = grad_hidden.T.reshape(COLS, BS, TOK)
    corners = [v[0, :8] for v in (gate_t, up_t, hidden, a[0])]
    place = call(
        place_kernel, jax.ShapeDtypeStruct((BLOCKS,), jnp.int32), [SMEM] + [ANY] * 4, SMEM,
        [pltpu.SMEM((NX * NZ,), jnp.int32)],
    )(block_owner, *corners)
    ac = swap(a, "core")
    far, place = lax.optimization_barrier((far, place))
    b = spread(far, "y")
    bc = swap(b, "core")

    halves = [jax.ShapeDtypeStruct((count, 2 * BS, BS), bf16) for count in (NX * NZ, NX * 4, NX * 4)]
    first, send, keep = call(
        block_kernel, halves, [ANY] * 7 + [SMEM, SMEM], [ANY] * 3,
        [
            pltpu.VMEM((ROWS, BS, TOK), bf16),
            pltpu.VMEM((COLS, 2 * BS, KB * BS), bf16),
            pltpu.VMEM((COLS, BS, TOK), bf16),
            pltpu.VMEM((KB * BS, TOK), bf16),
            pltpu.VMEM((NX * NZ * CAP, 2 * BS, BS), bf16),
            pltpu.SemaphoreType.DMA((16,)),
            pltpu.SemaphoreType.DMA((3 * COLS,)),
            pltpu.SemaphoreType.DMA((3,)),
        ],
        flops=8 * BLOCKS * BS * BS * TOK, bytes_accessed=14 * 2**20,
    )(a, ac, b, bc, gate_t, up_t, hidden, block_rows, place)

    def over_x(value):
        return lax.all_to_all(value.reshape(NX, -1, BS), "x", 0, 0, tiled=True)

    got = swap(send.reshape(-1, BS), "z2")
    first = over_x(first)
    second = (keep.reshape(-1, BS).astype(f32) + got.astype(f32)).astype(bf16)
    half = first.shape[1] // 2
    send, first = call(
        sum_kernel, (jax.ShapeDtypeStruct((half, BS), bf16), jax.ShapeDtypeStruct((half, BS), f32)),
        [VMEM, ANY], (VMEM, VMEM), bytes_accessed=3 * 2**20,
    )(first, second)
    second = over_x(second)
    first = first + swap(send, "z2").astype(f32)
    second = jnp.sum(second.astype(f32), 0)
    both = jnp.concatenate([v.astype(bf16).reshape(4, 2 * BS, BS) for v in (first, second)], 1)
    got = lax.all_to_all(both, "z4", 0, 0, tiled=True)
    return jnp.sum(got.astype(f32), 0).reshape(1, 1, CAP, 2, BS, BS)


def solution(mesh):
    fine = Mesh(mesh.devices.reshape(tuple(AXES.values())), tuple(AXES))
    dp, tensor = ("z4", "z2", "x"), ("y", "zh", "core")
    in_specs = (
        P(dp, tensor),
        P(dp, tensor),
        P(tensor, None, None, None),
        P(tensor, None, None, None),
        P(tensor, None),
        P(tensor, None),
    )
    out_specs = P(tensor, dp, None, None, None, None)
    return jax.shard_map(body, mesh=fine, in_specs=in_specs, out_specs=out_specs, check_vma=False)
```

```python
import functools

import jax
import jax.numpy as jnp
from jax import lax
from jax.experimental import pallas as pl
from jax.experimental.pallas import tpu as pltpu
from jax.sharding import Mesh, PartitionSpec as P

BS = 128
KB = 8
COLS = 7
BLOCKS = COLS * KB
TOK = 512
ROWS = 32
NX, NZ, CAP = 4, 8, 2
AXES = {"z8": 2, "z4": 2, "z2": 2, "x": 4, "y": 4, "zh": 2, "core": 2}
VMEM = pl.BlockSpec(memory_space=pltpu.VMEM)
HBM = pl.BlockSpec(memory_space=pltpu.HBM)
ANY = pl.BlockSpec(memory_space=pl.ANY)
SMEM = pl.BlockSpec(memory_space=pltpu.SMEM)


def swap(value, axis):
    return lax.ppermute(value, axis, [(0, 1), (1, 0)])


def shift(value, axis, step):
    size = AXES[axis]
    return lax.ppermute(value, axis, [(i, (i + step) % size) for i in range(size)])


def spread(value, axis):
    return lax.all_to_all(jnp.broadcast_to(value[None], (AXES[axis],) + value.shape), axis, 0, 0, tiled=True)


def call(kernel, out_shape, in_specs, out_specs, scratch=(), flops=0, bytes_accessed=0):
    return pl.pallas_call(
        kernel,
        out_shape=out_shape,
        in_specs=in_specs,
        out_specs=out_specs,
        scratch_shapes=list(scratch),
        compiler_params=pltpu.CompilerParams(vmem_limit_bytes=40 * 1024 * 1024),
        cost_estimate=pl.CostEstimate(flops=flops, bytes_accessed=bytes_accessed, transcendentals=0),
    )


def place_kernel(owner_ref, gate_ref, up_ref, hidden_ref, near_ref, place_ref, seen_ref):
    my_x = lax.axis_index("x")
    my_z = lax.axis_index("z8") * 4 + lax.axis_index("z4") * 2 + lax.axis_index("z2")

    def clear(i, carry):
        seen_ref[i] = jnp.int32(0)
        return carry

    lax.fori_loop(0, NX * NZ, clear, 0)

    def place(i, carry):
        owner = owner_ref[i // KB, i % KB]
        slot = seen_ref[owner]
        seen_ref[owner] = slot + 1
        x = (owner % NX - my_x + NX) % NX
        z = (owner // NX) ^ my_z
        other = z & 1
        rest = (z & 2) + (z >> 2)
        first = x * NZ + other * 4 + rest
        second = NX * NZ + (1 - other) * (NX * 4) + x * 4 + rest
        place_ref[i] = jnp.where(slot == 0, first, second)
        return carry

    lax.fori_loop(0, BLOCKS, place, 0)


def block_kernel(
    a_ref, ac_ref, b_ref, bc_ref, gate_ref, up_ref, hidden_ref, rows_ref, place_ref,
    send_ref, first0_ref, first1_ref, first2_ref, first3_ref, keep_ref, x_ref, w_ref, h_ref, picked_ref, out_ref, x_sem, w_sem, out_sem,
):
    zh = lax.axis_index("zh")
    core = lax.axis_index("core")
    x_copies = []
    for i, (ref, z, c) in enumerate(
        ((a_ref, zh, core), (ac_ref, zh, 1 - core), (b_ref, 1 - zh, core), (bc_ref, 1 - zh, 1 - core))
    ):
        for y in range(4):
            at = (y * 4 + z * 2 + c) * 2
            x_copies.append(pltpu.make_async_copy(ref.at[y], x_ref.at[pl.ds(at, 2)], x_sem.at[i * 4 + y]))
    w_copies = []
    for c in range(COLS):
        w_copies.append((
            pltpu.make_async_copy(gate_ref.at[c], w_ref.at[c, pl.ds(0, BS)], w_sem.at[3 * c]),
            pltpu.make_async_copy(up_ref.at[c], w_ref.at[c, pl.ds(BS, BS)], w_sem.at[3 * c + 1]),
            pltpu.make_async_copy(hidden_ref.at[c], h_ref.at[c], w_sem.at[3 * c + 2]),
        ))
    for copy in x_copies:
        copy.start()
    for copies in w_copies:
        for copy in copies:
            copy.start()
    out_ref[...] = jnp.zeros_like(out_ref)
    for copy in x_copies:
        copy.wait()
    for c in range(COLS):
        now_ref = picked_ref.at[c % 2]
        for k in range(KB):
            now_ref[k * BS:(k + 1) * BS] = x_ref[rows_ref[c, k]]
        for copy in w_copies[c]:
            copy.wait()
        picked = now_ref[...]
        pre = jnp.dot(w_ref[c], picked, preferred_element_type=jnp.float32)
        gate, up = pre[:BS], pre[BS:]
        s = jax.nn.sigmoid(gate)
        h = h_ref[c].astype(jnp.float32)
        grad_gate = (h * up * (s * (1.0 + gate * (1.0 - s)))).astype(jnp.bfloat16)
        grad_up = (h * (gate * s)).astype(jnp.bfloat16)
        value = lax.dot_general(
            picked, jnp.concatenate([grad_gate, grad_up], 0), (((1,), (1,)), ((), ())),
            preferred_element_type=jnp.float32,
        ).astype(jnp.bfloat16)
        for k in range(KB):
            for m in range(2):
                out_ref[place_ref[c * KB + k], m * BS:(m + 1) * BS] = value[k * BS:(k + 1) * BS, m * BS:(m + 1) * BS]
    places = [NX * NZ] + [i * NZ for i in range(NX)] + [NX * NZ + NX * 4]
    out_copies = []
    for i, ref in enumerate((send_ref, first0_ref, first1_ref, first2_ref, first3_ref, keep_ref)):
        out_copies.append(pltpu.make_async_copy(out_ref.at[pl.ds(places[i], ref.shape[0])], ref, out_sem.at[i]))
    for copy in out_copies:
        copy.start()
    for copy in out_copies:
        copy.wait()


def body(x_panel, grad_hidden, gate_blocks, up_blocks, block_rows, block_owner):
    bf16, f32 = jnp.bfloat16, jnp.float32
    own = x_panel.T.reshape(2, BS, TOK)
    far = swap(own, "zh")
    a = spread(own, "y")
    gate_t, up_t = (w.transpose(0, 3, 1, 2).reshape(COLS, BS, KB * BS) for w in (gate_blocks, up_blocks))
    hidden = grad_hidden.T.reshape(COLS, BS, TOK)
    corners = [v[0, :8] for v in (gate_t, up_t, hidden, a[0])]
    place = call(
        place_kernel, jax.ShapeDtypeStruct((BLOCKS,), jnp.int32), [SMEM] + [ANY] * 4, SMEM,
        [pltpu.SMEM((NX * NZ,), jnp.int32)],
    )(block_owner, *corners)
    ac = swap(a, "core")
    far, place = lax.optimization_barrier((far, place))
    b = spread(far, "y")
    bc = swap(b, "core")

    counts = (NX * 4, NZ, NZ, NZ, NZ, NX * 4)
    send, *firsts, keep = call(
        block_kernel, [jax.ShapeDtypeStruct((count, 2 * BS, BS), bf16) for count in counts],
        [HBM] * 7 + [SMEM, SMEM], [ANY] * 6,
        [
            pltpu.VMEM((ROWS, BS, TOK), bf16),
            pltpu.VMEM((COLS, 2 * BS, KB * BS), bf16),
            pltpu.VMEM((COLS, BS, TOK), bf16),
            pltpu.VMEM((2, KB * BS, TOK), bf16),
            pltpu.VMEM((NX * NZ * CAP, 2 * BS, BS), bf16),
            pltpu.SemaphoreType.DMA((16,)),
            pltpu.SemaphoreType.DMA((3 * COLS,)),
            pltpu.SemaphoreType.DMA((6,)),
        ],
        flops=8 * BLOCKS * BS * BS * TOK, bytes_accessed=14 * 2**20,
    )(a, ac, b, bc, gate_t, up_t, hidden, block_rows, place)

    def over_x(parts):
        parts = [parts[0]] + [shift(parts[i], "x", i) for i in range(1, NX)]
        return sum(part.astype(f32) for part in parts)

    def halve(keep, axis):
        half = keep.shape[0] // 2
        return keep[:half] + swap(keep[half:].astype(bf16), axis).astype(f32)

    got = swap(send.reshape(-1, BS), "z2").reshape(NX, -1, BS)
    keep = keep.reshape(NX, -1, BS)
    first = over_x([part.reshape(-1, BS) for part in firsts])
    second = over_x([(keep[i].astype(f32) + got[i].astype(f32)).astype(bf16) for i in range(NX)])
    first = halve(halve(halve(first, "z2"), "z4"), "z8")
    second = halve(halve(second, "z4"), "z8")
    return jnp.concatenate([first, second], 0).reshape(1, 1, CAP, 2, BS, BS)


def solution(mesh):
    fine = Mesh(mesh.devices.reshape(tuple(AXES.values())), tuple(AXES))
    dp, tensor = ("z8", "z4", "z2", "x"), ("y", "zh", "core")
    in_specs = (
        P(dp, tensor),
        P(dp, tensor),
        P(tensor, None, None, None),
        P(tensor, None, None, None),
        P(tensor, None),
        P(tensor, None),
    )
    out_specs = P(tensor, dp, None, None, None, None)
    return jax.shard_map(body, mesh=fine, in_specs=in_specs, out_specs=out_specs, check_vma=False)
```

```python
import functools

import jax
import jax.numpy as jnp
from jax import lax
from jax.experimental import pallas as pl
from jax.experimental.pallas import tpu as pltpu
from jax.sharding import Mesh, PartitionSpec as P

BS = 128
KB = 8
COLS = 7
BLOCKS = COLS * KB
TOK = 512
ROWS = 32
NX, NZ, CAP = 4, 8, 2
VMEM_MIB = 40
AXES = {"z8": 2, "z4": 2, "z2": 2, "x": 4, "y": 4, "zh": 2, "core": 2}
VMEM = pl.BlockSpec(memory_space=pltpu.VMEM)
HBM = pl.BlockSpec(memory_space=pltpu.HBM)
ANY = pl.BlockSpec(memory_space=pl.ANY)
SMEM = pl.BlockSpec(memory_space=pltpu.SMEM)


def swap(value, axis):
    return lax.ppermute(value, axis, [(0, 1), (1, 0)])


def shift(value, axis, step):
    size = AXES[axis]
    return lax.ppermute(value, axis, [(i, (i + step) % size) for i in range(size)])


def spread(value, axis):
    return lax.all_to_all(jnp.broadcast_to(value[None], (AXES[axis],) + value.shape), axis, 0, 0, tiled=True)


def call(kernel, out_shape, in_specs, out_specs, scratch=(), flops=0, bytes_accessed=0, vmem_mib=16):
    return pl.pallas_call(
        kernel,
        out_shape=out_shape,
        in_specs=in_specs,
        out_specs=out_specs,
        scratch_shapes=list(scratch),
        compiler_params=pltpu.CompilerParams(vmem_limit_bytes=vmem_mib * 2**20),
        cost_estimate=pl.CostEstimate(flops=flops, bytes_accessed=bytes_accessed, transcendentals=0),
    )


def place_kernel(owner_ref, gate_ref, up_ref, hidden_ref, near_ref, place_ref, seen_ref):
    my_x = lax.axis_index("x")
    my_z = lax.axis_index("z8") * 4 + lax.axis_index("z4") * 2 + lax.axis_index("z2")

    def clear(i, carry):
        seen_ref[i] = jnp.int32(0)
        return carry

    lax.fori_loop(0, NX * NZ, clear, 0)

    def place(i, carry):
        owner = owner_ref[i // KB, i % KB]
        slot = seen_ref[owner]
        seen_ref[owner] = slot + 1
        x = (owner % NX - my_x + NX) % NX
        z = (owner // NX) ^ my_z
        other = z & 1
        rest = (z & 2) + (z >> 2)
        first = x * NZ + other * 4 + rest
        second = NX * NZ + (1 - other) * (NX * 4) + x * 4 + rest
        place_ref[i] = jnp.where(slot == 0, first, second)
        return carry

    lax.fori_loop(0, BLOCKS, place, 0)


def block_kernel(
    a_ref, ac_ref, b_ref, bc_ref, gate_ref, up_ref, hidden_ref, rows_ref, place_ref,
    out_ref, send_ref, x_ref, w_ref, h_ref, picked_ref, x_sem, w_sem, out_sem,
):
    zh = lax.axis_index("zh")
    core = lax.axis_index("core")
    x_copies = []
    for i, (ref, z, c) in enumerate(
        ((a_ref, zh, core), (ac_ref, zh, 1 - core), (b_ref, 1 - zh, core), (bc_ref, 1 - zh, 1 - core))
    ):
        for y in range(4):
            at = (y * 4 + z * 2 + c) * 2
            x_copies.append(pltpu.make_async_copy(ref.at[y], x_ref.at[pl.ds(at, 2)], x_sem.at[i * 4 + y]))
    w_copies = []
    for c in range(COLS):
        w_copies.append((
            pltpu.make_async_copy(gate_ref.at[c], w_ref.at[c, pl.ds(0, BS)], w_sem.at[3 * c]),
            pltpu.make_async_copy(up_ref.at[c], w_ref.at[c, pl.ds(BS, BS)], w_sem.at[3 * c + 1]),
            pltpu.make_async_copy(hidden_ref.at[c], h_ref.at[c], w_sem.at[3 * c + 2]),
        ))
    for copy in x_copies:
        copy.start()
    for copies in w_copies:
        for copy in copies:
            copy.start()
    out_ref[...] = jnp.zeros_like(out_ref)
    for copy in x_copies:
        copy.wait()
    for c in range(COLS):
        now_ref = picked_ref.at[c % 2]
        for k in range(KB):
            now_ref[k * BS:(k + 1) * BS] = x_ref[rows_ref[c, k]]
        for copy in w_copies[c]:
            copy.wait()
        picked = now_ref[...]
        pre = jnp.dot(w_ref[c], picked, preferred_element_type=jnp.float32)
        gate, up = pre[:BS], pre[BS:]
        s = jax.nn.sigmoid(gate)
        h = h_ref[c].astype(jnp.float32)
        grad_gate = (h * up * (s * (1.0 + gate * (1.0 - s)))).astype(jnp.bfloat16)
        grad_up = (h * (gate * s)).astype(jnp.bfloat16)
        value = lax.dot_general(
            picked, jnp.concatenate([grad_gate, grad_up], 0), (((1,), (1,)), ((), ())),
            preferred_element_type=jnp.float32,
        ).astype(jnp.bfloat16)
        for k in range(KB):
            for m in range(2):
                out_ref[place_ref[c * KB + k], m * BS:(m + 1) * BS] = value[k * BS:(k + 1) * BS, m * BS:(m + 1) * BS]
    copy = pltpu.make_async_copy(out_ref.at[pl.ds(NX * NZ, NX * 4)], send_ref, out_sem)
    copy.start()
    copy.wait()


def split_kernel(out_ref, *refs):
    *refs, sem = refs
    copies = []
    for i, ref in enumerate(refs):
        copies.append(pltpu.make_async_copy(out_ref.at[pl.ds((i + 1) * NZ, NZ)], ref, sem.at[i]))
    for copy in copies:
        copy.start()
    for copy in copies:
        copy.wait()


def add_kernel(out_ref, got_ref, order1_ref, order2_ref, order3_ref, *refs):
    for i, ref in enumerate(refs):
        for j in range(4):
            at = i * 4 + j
            total = out_ref[NX * NZ + NX * 4 + at].astype(jnp.float32) + got_ref[at].astype(jnp.float32)
            ref[j] = total.astype(ref.dtype)


def sum_kernel(out_ref, got1_ref, got2_ref, got3_ref, order_ref, send_ref, keep_ref):
    for ref, at in ((keep_ref, 0), (send_ref, NZ // 2)):
        for i in range(NZ // 2):
            total = out_ref[at + i].astype(jnp.float32)
            for got_ref in (got1_ref, got2_ref, got3_ref):
                total += got_ref[at + i].astype(jnp.float32)
            ref[i] = total.astype(ref.dtype)


def body(x_panel, grad_hidden, gate_blocks, up_blocks, block_rows, block_owner):
    bf16, f32 = jnp.bfloat16, jnp.float32
    own = x_panel.T.reshape(2, BS, TOK)
    far = swap(own, "zh")
    a = spread(own, "y")
    gate_t, up_t = (w.transpose(0, 3, 1, 2).reshape(COLS, BS, KB * BS) for w in (gate_blocks, up_blocks))
    hidden = grad_hidden.T.reshape(COLS, BS, TOK)
    corners = [v[0, :8] for v in (gate_t, up_t, hidden, a[0])]
    place = call(
        place_kernel, jax.ShapeDtypeStruct((BLOCKS,), jnp.int32), [SMEM] + [ANY] * 4, SMEM,
        [pltpu.SMEM((NX * NZ,), jnp.int32)],
    )(block_owner, *corners)
    ac = swap(a, "core")
    far, place = lax.optimization_barrier((far, place))
    b = spread(far, "y")
    bc = swap(b, "core")

    def places(count):
        return jax.ShapeDtypeStruct((count, 2 * BS, BS), bf16)

    out, send = call(
        block_kernel, (places(NX * NZ * CAP), places(NX * 4)), [HBM] * 7 + [SMEM, SMEM], (VMEM, ANY),
        [
            pltpu.VMEM((ROWS, BS, TOK), bf16),
            pltpu.VMEM((COLS, 2 * BS, KB * BS), bf16),
            pltpu.VMEM((COLS, BS, TOK), bf16),
            pltpu.VMEM((2, KB * BS, TOK), bf16),
            pltpu.SemaphoreType.DMA((16,)),
            pltpu.SemaphoreType.DMA((3 * COLS,)),
            pltpu.SemaphoreType.DMA,
        ],
        flops=8 * BLOCKS * BS * BS * TOK, bytes_accessed=14 * 2**20, vmem_mib=VMEM_MIB,
    )(a, ac, b, bc, gate_t, up_t, hidden, block_rows, place)
    firsts = call(
        split_kernel, [places(NZ)] * (NX - 1), [VMEM], [ANY] * (NX - 1),
        [pltpu.SemaphoreType.DMA((NX - 1,))], bytes_accessed=3 * 2**20,
    )(out)

    def over_x(parts):
        return [shift(part, "x", i + 1) for i, part in enumerate(parts)]

    def halve(keep, axis):
        half = keep.shape[0] // 2
        return keep[:half] + swap(keep[half:].astype(bf16), axis).astype(f32)

    got = swap(send, "z2")
    first = over_x(firsts)
    kept, *seconds = call(
        add_kernel, [places(4)] * NX, [VMEM] * 2 + [ANY] * 3, [VMEM] * NX, bytes_accessed=3 * 2**20,
    )(out, got, *first)
    second = over_x(seconds)
    send, first = call(
        sum_kernel, (places(4), jax.ShapeDtypeStruct((4, 2 * BS, BS), f32)), [VMEM] * NX + [ANY], (VMEM, VMEM),
        bytes_accessed=3 * 2**20,
    )(out, *first, kept)
    first = first + swap(send, "z2").astype(f32)
    first = halve(halve(first, "z4"), "z8")
    second = kept.astype(f32) + sum(part.astype(f32) for part in second)
    second = halve(halve(second, "z4"), "z8")
    return jnp.concatenate([first, second], 0).reshape(1, 1, CAP, 2, BS, BS)


def solution(mesh):
    fine = Mesh(mesh.devices.reshape(tuple(AXES.values())), tuple(AXES))
    dp, tensor = ("z8", "z4", "z2", "x"), ("y", "zh", "core")
    in_specs = (
        P(dp, tensor),
        P(dp, tensor),
        P(tensor, None, None, None),
        P(tensor, None, None, None),
        P(tensor, None),
        P(tensor, None),
    )
    out_specs = P(tensor, dp, None, None, None, None)
    return jax.shard_map(body, mesh=fine, in_specs=in_specs, out_specs=out_specs, check_vma=False)
```

```python
import functools

import jax
import jax.numpy as jnp
from jax import lax
from jax.experimental import pallas as pl
from jax.experimental.pallas import tpu as pltpu
from jax.sharding import Mesh, PartitionSpec as P

BS = 128
KB = 8
COLS = 7
BLOCKS = COLS * KB
TOK = 512
ROWS = 32
NX, NZ, CAP = 4, 8, 2
VMEM_MIB = 60
AXES = {"z8": 2, "z4": 2, "z2": 2, "x": 4, "y": 4, "zh": 2, "core": 2}
VMEM = pl.BlockSpec(memory_space=pltpu.VMEM)
HBM = pl.BlockSpec(memory_space=pltpu.HBM)
ANY = pl.BlockSpec(memory_space=pl.ANY)
SMEM = pl.BlockSpec(memory_space=pltpu.SMEM)


def swap(value, axis):
    return lax.ppermute(value, axis, [(0, 1), (1, 0)])


def shift(value, axis, step):
    size = AXES[axis]
    return lax.ppermute(value, axis, [(i, (i + step) % size) for i in range(size)])


def spread(value, axis):
    return lax.all_to_all(jnp.broadcast_to(value[None], (AXES[axis],) + value.shape), axis, 0, 0, tiled=True)


def call(kernel, out_shape, in_specs, out_specs, scratch=(), flops=0, bytes_accessed=0, vmem_mib=16):
    return pl.pallas_call(
        kernel,
        out_shape=out_shape,
        in_specs=in_specs,
        out_specs=out_specs,
        scratch_shapes=list(scratch),
        compiler_params=pltpu.CompilerParams(vmem_limit_bytes=vmem_mib * 2**20),
        cost_estimate=pl.CostEstimate(flops=flops, bytes_accessed=bytes_accessed, transcendentals=0),
    )


def place_kernel(owner_ref, gate_ref, up_ref, hidden_ref, near_ref, place_ref, seen_ref):
    my_x = lax.axis_index("x")
    my_z = lax.axis_index("z8") * 4 + lax.axis_index("z4") * 2 + lax.axis_index("z2")

    def clear(i, carry):
        seen_ref[i] = jnp.int32(0)
        return carry

    lax.fori_loop(0, NX * NZ, clear, 0)

    def place(i, carry):
        owner = owner_ref[i // KB, i % KB]
        slot = seen_ref[owner]
        seen_ref[owner] = slot + 1
        x = owner % NX
        rel_x = (x - my_x + NX) % NX
        z = (owner // NX) ^ my_z
        other = z & 1
        rest = (z & 2) + (z >> 2)
        first = x * NZ + other * 4 + rest
        second = NX * NZ + (1 - other) * (NX * 4) + rel_x * 4 + rest
        place_ref[i] = jnp.where(slot == 0, first, second)
        return carry

    lax.fori_loop(0, BLOCKS, place, 0)


def block_kernel(
    a_ref, ac_ref, b_ref, bc_ref, gate_ref, up_ref, hidden_ref, rows_ref, place_ref,
    first_ref, send_ref, keep_ref, x_ref, w_ref, h_ref, picked_ref, act_ref, out_ref, x_sem, w_sem, out_sem,
):
    zh = lax.axis_index("zh")
    core = lax.axis_index("core")
    x_copies = []
    for i, (ref, z, c) in enumerate(
        ((a_ref, zh, core), (ac_ref, zh, 1 - core), (b_ref, 1 - zh, core), (bc_ref, 1 - zh, 1 - core))
    ):
        for y in range(4):
            at = (y * 4 + z * 2 + c) * 2
            x_copies.append(pltpu.make_async_copy(ref.at[y], x_ref.at[pl.ds(at, 2)], x_sem.at[i * 4 + y]))
    w_copies = []
    for c in range(COLS):
        w_copies.append((
            pltpu.make_async_copy(gate_ref.at[c], w_ref.at[c, pl.ds(0, BS)], w_sem.at[3 * c]),
            pltpu.make_async_copy(up_ref.at[c], w_ref.at[c, pl.ds(BS, BS)], w_sem.at[3 * c + 1]),
            pltpu.make_async_copy(hidden_ref.at[c], h_ref.at[c], w_sem.at[3 * c + 2]),
        ))
    for copy in x_copies:
        copy.start()
    for copies in w_copies:
        for copy in copies:
            copy.start()
    out_ref[...] = jnp.zeros_like(out_ref)
    for copy in x_copies:
        copy.wait()
    for c in range(COLS):
        now_ref = picked_ref.at[c]
        for k in range(KB):
            now_ref[k * BS:(k + 1) * BS] = x_ref[rows_ref[c, k]]
        for copy in w_copies[c]:
            copy.wait()
        pre = jnp.dot(w_ref[c], now_ref[...], preferred_element_type=jnp.float32)
        gate, up = pre[:BS], pre[BS:]
        s = jax.nn.sigmoid(gate)
        h = h_ref[c].astype(jnp.float32)
        act_ref[c, :BS] = (h * up * (s * (1.0 + gate * (1.0 - s)))).astype(jnp.bfloat16)
        act_ref[c, BS:] = (h * (gate * s)).astype(jnp.bfloat16)
    for c in range(COLS):
        value = lax.dot_general(
            picked_ref[c], act_ref[c], (((1,), (1,)), ((), ())), preferred_element_type=jnp.float32
        ).astype(jnp.bfloat16)
        for k in range(KB):
            for m in range(2):
                out_ref[place_ref[c * KB + k], m * BS:(m + 1) * BS] = value[k * BS:(k + 1) * BS, m * BS:(m + 1) * BS]
    out_copies = []
    for i, (ref, at) in enumerate(((send_ref, NX * NZ), (first_ref, 0), (keep_ref, NX * NZ + NX * 4))):
        out_copies.append(pltpu.make_async_copy(out_ref.at[pl.ds(at, ref.shape[0])], ref, out_sem.at[i]))
    for copy in out_copies:
        copy.start()
    for copy in out_copies:
        copy.wait()


def add_kernel(keep_ref, got_ref, *refs):
    for i, ref in enumerate(refs):
        for j in range(4):
            at = i * 4 + j
            ref[j] = (keep_ref[at].astype(jnp.float32) + got_ref[at].astype(jnp.float32)).astype(ref.dtype)


def sum_kernel(got_ref, order_ref, send_ref, keep_ref):
    for ref, at in ((keep_ref, 0), (send_ref, NZ // 2)):
        for i in range(NZ // 2):
            total = got_ref[at + i].astype(jnp.float32)
            for x in range(1, NX):
                total += got_ref[x * NZ + at + i].astype(jnp.float32)
            ref[i] = total.astype(ref.dtype)


def body(x_panel, grad_hidden, gate_blocks, up_blocks, block_rows, block_owner):
    bf16, f32 = jnp.bfloat16, jnp.float32
    own = x_panel.T.reshape(2, BS, TOK)
    far = swap(own, "zh")
    a = spread(own, "y")
    gate_t, up_t = (w.transpose(0, 3, 1, 2).reshape(COLS, BS, KB * BS) for w in (gate_blocks, up_blocks))
    hidden = grad_hidden.T.reshape(COLS, BS, TOK)
    corners = [v[0, :8] for v in (gate_t, up_t, hidden, a[0])]
    place = call(
        place_kernel, jax.ShapeDtypeStruct((BLOCKS,), jnp.int32), [SMEM] + [ANY] * 4, SMEM,
        [pltpu.SMEM((NX * NZ,), jnp.int32)],
    )(block_owner, *corners)
    ac = swap(a, "core")
    far, place = lax.optimization_barrier((far, place))
    b = spread(far, "y")
    bc = swap(b, "core")

    def places(count):
        return jax.ShapeDtypeStruct((count, 2 * BS, BS), bf16)

    first, send, keep = call(
        block_kernel, (places(NX * NZ), places(NX * 4), places(NX * 4)),
        [HBM] * 7 + [SMEM, SMEM], (HBM, ANY, HBM),
        [
            pltpu.VMEM((ROWS, BS, TOK), bf16),
            pltpu.VMEM((COLS, 2 * BS, KB * BS), bf16),
            pltpu.VMEM((COLS, BS, TOK), bf16),
            pltpu.VMEM((COLS, KB * BS, TOK), bf16),
            pltpu.VMEM((COLS, 2 * BS, TOK), bf16),
            pltpu.VMEM((NX * NZ * CAP, 2 * BS, BS), bf16),
            pltpu.SemaphoreType.DMA((16,)),
            pltpu.SemaphoreType.DMA((3 * COLS,)),
            pltpu.SemaphoreType.DMA((3,)),
        ],
        flops=8 * BLOCKS * BS * BS * TOK, bytes_accessed=14 * 2**20, vmem_mib=VMEM_MIB,
    )(a, ac, b, bc, gate_t, up_t, hidden, block_rows, place)
    def halve(keep, axis):
        half = keep.shape[0] // 2
        return keep[:half] + swap(keep[half:].astype(bf16), axis).astype(f32)

    got = swap(send, "z2")
    first = lax.all_to_all(first, "x", 0, 0, tiled=True)
    kept, *seconds = call(
        add_kernel, [places(4)] * NX, [VMEM] * 2, [VMEM] * NX, bytes_accessed=3 * 2**20,
    )(keep, got)
    second = [shift(seconds[i - 1], "x", i) for i in (1, 3, 2)]
    send, first = call(
        sum_kernel, (places(4), jax.ShapeDtypeStruct((4, 2 * BS, BS), f32)), [VMEM, ANY], (VMEM, VMEM),
        bytes_accessed=3 * 2**20,
    )(first, kept)
    first = first + swap(send, "z2").astype(f32)
    first = halve(halve(first, "z4"), "z8")
    second = kept.astype(f32) + sum(part.astype(f32) for part in second)
    second = halve(halve(second, "z4"), "z8")
    return jnp.concatenate([first, second], 0).reshape(1, 1, CAP, 2, BS, BS)


def solution(mesh):
    fine = Mesh(mesh.devices.reshape(tuple(AXES.values())), tuple(AXES))
    dp, tensor = ("z8", "z4", "z2", "x"), ("y", "zh", "core")
    in_specs = (
        P(dp, tensor),
        P(dp, tensor),
        P(tensor, None, None, None),
        P(tensor, None, None, None),
        P(tensor, None),
        P(tensor, None),
    )
    out_specs = P(tensor, dp, None, None, None, None)
    return jax.shard_map(body, mesh=fine, in_specs=in_specs, out_specs=out_specs, check_vma=False)
```

```python
import functools

import jax
import jax.numpy as jnp
from jax import lax
from jax.experimental import pallas as pl
from jax.experimental.pallas import tpu as pltpu
from jax.sharding import Mesh, PartitionSpec as P

BS = 128
KB = 8
COLS = 7
BLOCKS = COLS * KB
TOK = 512
ROWS = 32
NX, NZ, CAP = 4, 8, 2
VMEM_MIB = 60
AXES = {"z8": 2, "z4": 2, "z2": 2, "x": 4, "y": 4, "zh": 2, "core": 2}
VMEM = pl.BlockSpec(memory_space=pltpu.VMEM)
HBM = pl.BlockSpec(memory_space=pltpu.HBM)
ANY = pl.BlockSpec(memory_space=pl.ANY)
SMEM = pl.BlockSpec(memory_space=pltpu.SMEM)


def swap(value, axis):
    return lax.ppermute(value, axis, [(0, 1), (1, 0)])


def shift(value, axis, step):
    size = AXES[axis]
    return lax.ppermute(value, axis, [(i, (i + step) % size) for i in range(size)])


def spread(value, axis):
    return lax.all_to_all(jnp.broadcast_to(value[None], (AXES[axis],) + value.shape), axis, 0, 0, tiled=True)


def call(kernel, out_shape, in_specs, out_specs, scratch=(), flops=0, bytes_accessed=0, vmem_mib=16):
    return pl.pallas_call(
        kernel,
        out_shape=out_shape,
        in_specs=in_specs,
        out_specs=out_specs,
        scratch_shapes=list(scratch),
        compiler_params=pltpu.CompilerParams(vmem_limit_bytes=vmem_mib * 2**20),
        cost_estimate=pl.CostEstimate(flops=flops, bytes_accessed=bytes_accessed, transcendentals=0),
    )


def place_kernel(owner_ref, gate_ref, up_ref, hidden_ref, near_ref, place_ref, seen_ref):
    my_x = lax.axis_index("x")
    my_z = lax.axis_index("z8") * 4 + lax.axis_index("z4") * 2 + lax.axis_index("z2")

    def clear(i, carry):
        seen_ref[i] = jnp.int32(0)
        return carry

    lax.fori_loop(0, NX * NZ, clear, 0)

    def place(i, carry):
        owner = owner_ref[i // KB, i % KB]
        slot = seen_ref[owner]
        seen_ref[owner] = slot + 1
        x = owner % NX
        rel_x = (x - my_x + NX) % NX
        z = (owner // NX) ^ my_z
        other = z & 1
        rest = (z & 2) + (z >> 2)
        first = x * NZ + other * 4 + rest
        second = NX * NZ + (1 - other) * (NX * 4) + rel_x * 4 + rest
        place_ref[i] = jnp.where(slot == 0, first, second)
        return carry

    lax.fori_loop(0, BLOCKS, place, 0)


def block_kernel(
    a_ref, ac_ref, b_ref, bc_ref, gate_ref, up_ref, hidden_ref, rows_ref, place_ref,
    first_ref, send_ref, keep_ref, x_ref, w_ref, h_ref, picked_ref, act_ref, out_ref, x_sem, w_sem, out_sem,
):
    zh = lax.axis_index("zh")
    core = lax.axis_index("core")
    x_copies = []
    for i, (ref, z, c) in enumerate(
        ((a_ref, zh, core), (ac_ref, zh, 1 - core), (b_ref, 1 - zh, core), (bc_ref, 1 - zh, 1 - core))
    ):
        for y in range(4):
            at = (y * 4 + z * 2 + c) * 2
            x_copies.append(pltpu.make_async_copy(ref.at[y], x_ref.at[pl.ds(at, 2)], x_sem.at[i * 4 + y]))
    w_copies = []
    for c in range(COLS):
        w_copies.append((
            pltpu.make_async_copy(gate_ref.at[c], w_ref.at[c, pl.ds(0, BS)], w_sem.at[3 * c]),
            pltpu.make_async_copy(up_ref.at[c], w_ref.at[c, pl.ds(BS, BS)], w_sem.at[3 * c + 1]),
            pltpu.make_async_copy(hidden_ref.at[c], h_ref.at[c], w_sem.at[3 * c + 2]),
        ))
    for copy in x_copies:
        copy.start()
    for copies in w_copies:
        for copy in copies:
            copy.start()
    out_ref[...] = jnp.zeros_like(out_ref)
    for copy in x_copies:
        copy.wait()
    for c in range(COLS):
        now_ref = picked_ref.at[c]
        for k in range(KB):
            now_ref[k * BS:(k + 1) * BS] = x_ref[rows_ref[c, k]]
        for copy in w_copies[c]:
            copy.wait()
        pre = jnp.dot(w_ref[c], now_ref[...], preferred_element_type=jnp.float32)
        gate, up = pre[:BS], pre[BS:]
        s = jax.nn.sigmoid(gate)
        h = h_ref[c].astype(jnp.float32)
        act_ref[c, :BS] = (h * up * (s * (1.0 + gate * (1.0 - s)))).astype(jnp.bfloat16)
        act_ref[c, BS:] = (h * (gate * s)).astype(jnp.bfloat16)
    for c in range(COLS):
        value = lax.dot_general(
            picked_ref[c], act_ref[c], (((1,), (1,)), ((), ())), preferred_element_type=jnp.float32
        ).astype(jnp.bfloat16)
        for k in range(KB):
            for m in range(2):
                out_ref[place_ref[c * KB + k], m * BS:(m + 1) * BS] = value[k * BS:(k + 1) * BS, m * BS:(m + 1) * BS]
    out_copies = []
    for i, (ref, at) in enumerate(((send_ref, NX * NZ), (first_ref, 0), (keep_ref, NX * NZ + NX * 4))):
        out_copies.append(pltpu.make_async_copy(out_ref.at[pl.ds(at, ref.shape[0])], ref, out_sem.at[i]))
    for copy in out_copies:
        copy.start()
    for copy in out_copies:
        copy.wait()


def add_kernel(keep_ref, got_ref, order_ref, *refs):
    for i, ref in enumerate(refs):
        for j in range(4):
            at = i * 4 + j
            ref[j] = (keep_ref[at].astype(jnp.float32) + got_ref[at].astype(jnp.float32)).astype(ref.dtype)


def sum_kernel(got_ref, send_ref, keep_ref):
    for ref, at in ((keep_ref, 0), (send_ref, NZ // 2)):
        for i in range(NZ // 2):
            total = got_ref[at + i].astype(jnp.float32)
            for x in range(1, NX):
                total += got_ref[x * NZ + at + i].astype(jnp.float32)
            ref[i] = total.astype(ref.dtype)


def body(x_panel, grad_hidden, gate_blocks, up_blocks, block_rows, block_owner):
    bf16, f32 = jnp.bfloat16, jnp.float32
    own = x_panel.T.reshape(2, BS, TOK)
    far = swap(own, "zh")
    a = spread(own, "y")
    gate_t, up_t = (w.transpose(0, 3, 1, 2).reshape(COLS, BS, KB * BS) for w in (gate_blocks, up_blocks))
    hidden = grad_hidden.T.reshape(COLS, BS, TOK)
    corners = [v[0, :8] for v in (gate_t, up_t, hidden, a[0])]
    place = call(
        place_kernel, jax.ShapeDtypeStruct((BLOCKS,), jnp.int32), [SMEM] + [ANY] * 4, SMEM,
        [pltpu.SMEM((NX * NZ,), jnp.int32)],
    )(block_owner, *corners)
    ac = swap(a, "core")
    far, place = lax.optimization_barrier((far, place))
    b = spread(far, "y")
    bc = swap(b, "core")

    def places(count):
        return jax.ShapeDtypeStruct((count, 2 * BS, BS), bf16)

    first, send, keep = call(
        block_kernel, (places(NX * NZ), places(NX * 4), places(NX * 4)),
        [HBM] * 7 + [SMEM, SMEM], (HBM, ANY, HBM),
        [
            pltpu.VMEM((ROWS, BS, TOK), bf16),
            pltpu.VMEM((COLS, 2 * BS, KB * BS), bf16),
            pltpu.VMEM((COLS, BS, TOK), bf16),
            pltpu.VMEM((COLS, KB * BS, TOK), bf16),
            pltpu.VMEM((COLS, 2 * BS, TOK), bf16),
            pltpu.VMEM((NX * NZ * CAP, 2 * BS, BS), bf16),
            pltpu.SemaphoreType.DMA((16,)),
            pltpu.SemaphoreType.DMA((3 * COLS,)),
            pltpu.SemaphoreType.DMA((3,)),
        ],
        flops=8 * BLOCKS * BS * BS * TOK, bytes_accessed=14 * 2**20, vmem_mib=VMEM_MIB,
    )(a, ac, b, bc, gate_t, up_t, hidden, block_rows, place)
    def halve(keep, axis):
        half = keep.shape[0] // 2
        return keep[:half] + swap(keep[half:].astype(bf16), axis).astype(f32)

    got = swap(send, "z2")
    first = lax.all_to_all(first, "x", 0, 0, tiled=True)
    send, first = call(
        sum_kernel, (places(4), jax.ShapeDtypeStruct((4, 2 * BS, BS), f32)), [VMEM], (VMEM, VMEM),
        bytes_accessed=3 * 2**20,
    )(first)
    got_first = swap(send, "z2")
    kept, *seconds = call(
        add_kernel, [places(4)] * NX, [VMEM] * 2 + [ANY], [VMEM] * NX, bytes_accessed=3 * 2**20,
    )(keep, got, got_first)
    second = [shift(seconds[i - 1], "x", i) for i in (1, 3, 2)]
    first = first + got_first.astype(f32)
    first = halve(halve(first, "z4"), "z8")
    second = kept.astype(f32) + sum(part.astype(f32) for part in second)
    second = halve(halve(second, "z4"), "z8")
    return jnp.concatenate([first, second], 0).reshape(1, 1, CAP, 2, BS, BS)


def solution(mesh):
    fine = Mesh(mesh.devices.reshape(tuple(AXES.values())), tuple(AXES))
    dp, tensor = ("z8", "z4", "z2", "x"), ("y", "zh", "core")
    in_specs = (
        P(dp, tensor),
        P(dp, tensor),
        P(tensor, None, None, None),
        P(tensor, None, None, None),
        P(tensor, None),
        P(tensor, None),
    )
    out_specs = P(tensor, dp, None, None, None, None)
    return jax.shard_map(body, mesh=fine, in_specs=in_specs, out_specs=out_specs, check_vma=False)
```

```python
import functools

import jax
import jax.numpy as jnp
from jax import lax
from jax.experimental import pallas as pl
from jax.experimental.pallas import tpu as pltpu
from jax.sharding import Mesh, PartitionSpec as P

BS = 128
KB = 8
COLS = 7
BLOCKS = COLS * KB
TOK = 512
ROWS = 32
NX, NZ, CAP = 4, 8, 2
VMEM_MIB = 60
AXES = {"z8": 2, "z4": 2, "z2": 2, "x": 4, "y": 4, "zh": 2, "core": 2}
VMEM = pl.BlockSpec(memory_space=pltpu.VMEM)
HBM = pl.BlockSpec(memory_space=pltpu.HBM)
ANY = pl.BlockSpec(memory_space=pl.ANY)
SMEM = pl.BlockSpec(memory_space=pltpu.SMEM)


def swap(value, axis):
    return lax.ppermute(value, axis, [(0, 1), (1, 0)])


def shift(value, axis, step):
    size = AXES[axis]
    return lax.ppermute(value, axis, [(i, (i + step) % size) for i in range(size)])


def spread(value, axis):
    return lax.all_to_all(jnp.broadcast_to(value[None], (AXES[axis],) + value.shape), axis, 0, 0, tiled=True)


def call(kernel, out_shape, in_specs, out_specs, scratch=(), flops=0, bytes_accessed=0, vmem_mib=16):
    return pl.pallas_call(
        kernel,
        out_shape=out_shape,
        in_specs=in_specs,
        out_specs=out_specs,
        scratch_shapes=list(scratch),
        compiler_params=pltpu.CompilerParams(vmem_limit_bytes=vmem_mib * 2**20),
        cost_estimate=pl.CostEstimate(flops=flops, bytes_accessed=bytes_accessed, transcendentals=0),
    )


def place_kernel(owner_ref, gate_ref, up_ref, hidden_ref, near_ref, place_ref, seen_ref):
    my_x = lax.axis_index("x")
    my_z = lax.axis_index("z8") * 4 + lax.axis_index("z4") * 2 + lax.axis_index("z2")

    def clear(i, carry):
        seen_ref[i] = jnp.int32(0)
        return carry

    lax.fori_loop(0, NX * NZ, clear, 0)

    def place(i, carry):
        owner = owner_ref[i // KB, i % KB]
        slot = seen_ref[owner]
        seen_ref[owner] = slot + 1
        x = (owner % NX - my_x + NX) % NX
        z = (owner // NX) ^ my_z
        other = z & 1
        rest = (z & 2) + (z >> 2)
        first = x * NZ + other * 4 + rest
        second = NX * NZ + (1 - other) * (NX * 4) + x * 4 + rest
        place_ref[i] = jnp.where(slot == 0, first, second)
        return carry

    lax.fori_loop(0, BLOCKS, place, 0)


def block_kernel(
    a_ref, ac_ref, b_ref, bc_ref, gate_ref, up_ref, hidden_ref, rows_ref, place_ref,
    send_ref, first0_ref, first1_ref, first2_ref, first3_ref, keep_ref, x_ref, w_ref, h_ref, picked_ref, out_ref, x_sem, w_sem, out_sem,
):
    zh = lax.axis_index("zh")
    core = lax.axis_index("core")
    x_copies = []
    for i, (ref, z, c) in enumerate(
        ((a_ref, zh, core), (ac_ref, zh, 1 - core), (b_ref, 1 - zh, core), (bc_ref, 1 - zh, 1 - core))
    ):
        for y in range(4):
            at = (y * 4 + z * 2 + c) * 2
            x_copies.append(pltpu.make_async_copy(ref.at[y], x_ref.at[pl.ds(at, 2)], x_sem.at[i * 4 + y]))
    w_copies = []
    for c in range(COLS):
        w_copies.append((
            pltpu.make_async_copy(gate_ref.at[c], w_ref.at[c, pl.ds(0, BS)], w_sem.at[3 * c]),
            pltpu.make_async_copy(up_ref.at[c], w_ref.at[c, pl.ds(BS, BS)], w_sem.at[3 * c + 1]),
            pltpu.make_async_copy(hidden_ref.at[c], h_ref.at[c], w_sem.at[3 * c + 2]),
        ))
    for copy in x_copies:
        copy.start()
    for copies in w_copies:
        for copy in copies:
            copy.start()
    out_ref[...] = jnp.zeros_like(out_ref)
    for copy in x_copies:
        copy.wait()
    for c in range(COLS):
        now_ref = picked_ref.at[c % 2]
        for k in range(KB):
            now_ref[k * BS:(k + 1) * BS] = x_ref[rows_ref[c, k]]
        for copy in w_copies[c]:
            copy.wait()
        picked = now_ref[...]
        pre = jnp.dot(w_ref[c], picked, preferred_element_type=jnp.float32)
        gate, up = pre[:BS], pre[BS:]
        s = jax.nn.sigmoid(gate)
        h = h_ref[c].astype(jnp.float32)
        grad_gate = (h * up * (s * (1.0 + gate * (1.0 - s)))).astype(jnp.bfloat16)
        grad_up = (h * (gate * s)).astype(jnp.bfloat16)
        value = lax.dot_general(
            picked, jnp.concatenate([grad_gate, grad_up], 0), (((1,), (1,)), ((), ())),
            preferred_element_type=jnp.float32,
        ).astype(jnp.bfloat16)
        for k in range(KB):
            for m in range(2):
                out_ref[place_ref[c * KB + k], m * BS:(m + 1) * BS] = value[k * BS:(k + 1) * BS, m * BS:(m + 1) * BS]
    places = [NX * NZ] + [i * NZ for i in range(NX)] + [NX * NZ + NX * 4]
    out_copies = []
    for i, ref in enumerate((send_ref, first0_ref, first1_ref, first2_ref, first3_ref, keep_ref)):
        out_copies.append(pltpu.make_async_copy(out_ref.at[pl.ds(places[i], ref.shape[0])], ref, out_sem.at[i]))
    for copy in out_copies:
        copy.start()
    for copy in out_copies:
        copy.wait()


def body(x_panel, grad_hidden, gate_blocks, up_blocks, block_rows, block_owner):
    bf16, f32 = jnp.bfloat16, jnp.float32
    own = x_panel.T.reshape(2, BS, TOK)
    far = swap(own, "zh")
    a = spread(own, "y")
    gate_t, up_t = (w.transpose(0, 3, 1, 2).reshape(COLS, BS, KB * BS) for w in (gate_blocks, up_blocks))
    hidden = grad_hidden.T.reshape(COLS, BS, TOK)
    corners = [v[0, :8] for v in (gate_t, up_t, hidden, a[0])]
    place = call(
        place_kernel, jax.ShapeDtypeStruct((BLOCKS,), jnp.int32), [SMEM] + [ANY] * 4, SMEM,
        [pltpu.SMEM((NX * NZ,), jnp.int32)],
    )(block_owner, *corners)
    ac = swap(a, "core")
    far, place = lax.optimization_barrier((far, place))
    b = spread(far, "y")
    bc = swap(b, "core")

    counts = (NX * 4, NZ, NZ, NZ, NZ, NX * 4)
    send, *firsts, keep = call(
        block_kernel, [jax.ShapeDtypeStruct((count, 2 * BS, BS), bf16) for count in counts],
        [HBM] * 7 + [SMEM, SMEM], [ANY] * 6,
        [
            pltpu.VMEM((ROWS, BS, TOK), bf16),
            pltpu.VMEM((COLS, 2 * BS, KB * BS), bf16),
            pltpu.VMEM((COLS, BS, TOK), bf16),
            pltpu.VMEM((2, KB * BS, TOK), bf16),
            pltpu.VMEM((NX * NZ * CAP, 2 * BS, BS), bf16),
            pltpu.SemaphoreType.DMA((16,)),
            pltpu.SemaphoreType.DMA((3 * COLS,)),
            pltpu.SemaphoreType.DMA((6,)),
        ],
        flops=8 * BLOCKS * BS * BS * TOK, bytes_accessed=14 * 2**20, vmem_mib=VMEM_MIB,
    )(a, ac, b, bc, gate_t, up_t, hidden, block_rows, place)

    def over_x(parts):
        parts = [parts[0]] + [shift(parts[i], "x", i) for i in (1, 3, 2)]
        return sum(part.astype(f32) for part in parts)

    def halve(keep, axis):
        half = keep.shape[0] // 2
        return keep[:half] + swap(keep[half:].astype(bf16), axis).astype(f32)

    got = swap(send.reshape(-1, BS), "z2").reshape(NX, -1, BS)
    keep = keep.reshape(NX, -1, BS)
    first = over_x([part.reshape(-1, BS) for part in firsts])
    second = over_x([(keep[i].astype(f32) + got[i].astype(f32)).astype(bf16) for i in range(NX)])
    first = halve(halve(halve(first, "z2"), "z4"), "z8")
    second = halve(halve(second, "z4"), "z8")
    return jnp.concatenate([first, second], 0).reshape(1, 1, CAP, 2, BS, BS)


def solution(mesh):
    fine = Mesh(mesh.devices.reshape(tuple(AXES.values())), tuple(AXES))
    dp, tensor = ("z8", "z4", "z2", "x"), ("y", "zh", "core")
    in_specs = (
        P(dp, tensor),
        P(dp, tensor),
        P(tensor, None, None, None),
        P(tensor, None, None, None),
        P(tensor, None),
        P(tensor, None),
    )
    out_specs = P(tensor, dp, None, None, None, None)
    return jax.shard_map(body, mesh=fine, in_specs=in_specs, out_specs=out_specs, check_vma=False)
```

```python
import functools

import jax
import jax.numpy as jnp
from jax import lax
from jax.experimental import pallas as pl
from jax.experimental.pallas import tpu as pltpu
from jax.sharding import Mesh, PartitionSpec as P

BS = 128
KB = 8
COLS = 7
BLOCKS = COLS * KB
TOK = 512
ROWS = 32
NX, NZ, CAP = 4, 8, 2
VMEM_MIB = 50
AXES = {"z8": 2, "z4": 2, "z2": 2, "x": 4, "y": 4, "zh": 2, "core": 2}
VMEM = pl.BlockSpec(memory_space=pltpu.VMEM)
HBM = pl.BlockSpec(memory_space=pltpu.HBM)
ANY = pl.BlockSpec(memory_space=pl.ANY)
SMEM = pl.BlockSpec(memory_space=pltpu.SMEM)


def swap(value, axis):
    return lax.ppermute(value, axis, [(0, 1), (1, 0)])


def shift(value, axis, step):
    size = AXES[axis]
    return lax.ppermute(value, axis, [(i, (i + step) % size) for i in range(size)])


def spread(value, axis):
    return lax.all_to_all(jnp.broadcast_to(value[None], (AXES[axis],) + value.shape), axis, 0, 0, tiled=True)


def call(kernel, out_shape, in_specs, out_specs, scratch=(), flops=0, bytes_accessed=0, vmem_mib=16):
    return pl.pallas_call(
        kernel,
        out_shape=out_shape,
        in_specs=in_specs,
        out_specs=out_specs,
        scratch_shapes=list(scratch),
        compiler_params=pltpu.CompilerParams(vmem_limit_bytes=vmem_mib * 2**20),
        cost_estimate=pl.CostEstimate(flops=flops, bytes_accessed=bytes_accessed, transcendentals=0),
    )


def place_kernel(owner_ref, gate_ref, up_ref, hidden_ref, near_ref, place_ref, seen_ref):
    my_x = lax.axis_index("x")
    my_z = lax.axis_index("z8") * 4 + lax.axis_index("z4") * 2 + lax.axis_index("z2")

    def clear(i, carry):
        seen_ref[i] = jnp.int32(0)
        return carry

    lax.fori_loop(0, NX * NZ, clear, 0)

    def place(i, carry):
        owner = owner_ref[i // KB, i % KB]
        slot = seen_ref[owner]
        seen_ref[owner] = slot + 1
        x = (owner % NX - my_x + NX) % NX
        z = (owner // NX) ^ my_z
        other = z & 1
        rest = (z & 2) + (z >> 2)
        first = x * NZ + other * 4 + rest
        second = NX * NZ + (1 - other) * (NX * 4) + x * 4 + rest
        place_ref[i] = jnp.where(slot == 0, first, second)
        return carry

    lax.fori_loop(0, BLOCKS, place, 0)


def block_kernel(
    a_ref, ac_ref, b_ref, bc_ref, gate_ref, up_ref, hidden_ref, rows_ref, place_ref,
    send_ref, first0_ref, first1_ref, first2_ref, first3_ref, keep_ref, x_ref, w_ref, h_ref, picked_ref, act_ref, out_ref, x_sem, w_sem, out_sem,
):
    zh = lax.axis_index("zh")
    core = lax.axis_index("core")
    x_copies = []
    for i, (ref, z, c) in enumerate(
        ((a_ref, zh, core), (ac_ref, zh, 1 - core), (b_ref, 1 - zh, core), (bc_ref, 1 - zh, 1 - core))
    ):
        for y in range(4):
            at = (y * 4 + z * 2 + c) * 2
            x_copies.append(pltpu.make_async_copy(ref.at[y], x_ref.at[pl.ds(at, 2)], x_sem.at[i * 4 + y]))
    w_copies = []
    for c in range(COLS):
        w_copies.append((
            pltpu.make_async_copy(gate_ref.at[c], w_ref.at[c, pl.ds(0, BS)], w_sem.at[3 * c]),
            pltpu.make_async_copy(up_ref.at[c], w_ref.at[c, pl.ds(BS, BS)], w_sem.at[3 * c + 1]),
            pltpu.make_async_copy(hidden_ref.at[c], h_ref.at[c], w_sem.at[3 * c + 2]),
        ))
    for copy in x_copies:
        copy.start()
    for copies in w_copies:
        for copy in copies:
            copy.start()
    out_ref[...] = jnp.zeros_like(out_ref)
    for copy in x_copies:
        copy.wait()
    for c in range(COLS):
        now_ref = picked_ref.at[c]
        for k in range(KB):
            now_ref[k * BS:(k + 1) * BS] = x_ref[rows_ref[c, k]]
        for copy in w_copies[c]:
            copy.wait()
        pre = jnp.dot(w_ref[c], now_ref[...], preferred_element_type=jnp.float32)
        gate, up = pre[:BS], pre[BS:]
        s = jax.nn.sigmoid(gate)
        h = h_ref[c].astype(jnp.float32)
        act_ref[c, :BS] = (h * up * (s * (1.0 + gate * (1.0 - s)))).astype(jnp.bfloat16)
        act_ref[c, BS:] = (h * (gate * s)).astype(jnp.bfloat16)
    for c in range(COLS):
        value = lax.dot_general(
            picked_ref[c], act_ref[c], (((1,), (1,)), ((), ())), preferred_element_type=jnp.float32
        ).astype(jnp.bfloat16)
        for k in range(KB):
            for m in range(2):
                out_ref[place_ref[c * KB + k], m * BS:(m + 1) * BS] = value[k * BS:(k + 1) * BS, m * BS:(m + 1) * BS]
    places = [NX * NZ] + [i * NZ for i in range(NX)] + [NX * NZ + NX * 4]
    out_copies = []
    for i, ref in enumerate((send_ref, first0_ref, first1_ref, first2_ref, first3_ref, keep_ref)):
        out_copies.append(pltpu.make_async_copy(out_ref.at[pl.ds(places[i], ref.shape[0])], ref, out_sem.at[i]))
    for copy in out_copies:
        copy.start()
    for copy in out_copies:
        copy.wait()


def body(x_panel, grad_hidden, gate_blocks, up_blocks, block_rows, block_owner):
    bf16, f32 = jnp.bfloat16, jnp.float32
    own = x_panel.T.reshape(2, BS, TOK)
    far = swap(own, "zh")
    a = spread(own, "y")
    gate_t, up_t = (w.transpose(0, 3, 1, 2).reshape(COLS, BS, KB * BS) for w in (gate_blocks, up_blocks))
    hidden = grad_hidden.T.reshape(COLS, BS, TOK)
    corners = [v[0, :8] for v in (gate_t, up_t, hidden, a[0])]
    place = call(
        place_kernel, jax.ShapeDtypeStruct((BLOCKS,), jnp.int32), [SMEM] + [ANY] * 4, SMEM,
        [pltpu.SMEM((NX * NZ,), jnp.int32)],
    )(block_owner, *corners)
    ac = swap(a, "core")
    far, place = lax.optimization_barrier((far, place))
    b = spread(far, "y")
    bc = swap(b, "core")

    counts = (NX * 4, NZ, NZ, NZ, NZ, NX * 4)
    send, *firsts, keep = call(
        block_kernel, [jax.ShapeDtypeStruct((count, 2 * BS, BS), bf16) for count in counts],
        [HBM] * 7 + [SMEM, SMEM], [ANY] * 6,
        [
            pltpu.VMEM((ROWS, BS, TOK), bf16),
            pltpu.VMEM((COLS, 2 * BS, KB * BS), bf16),
            pltpu.VMEM((COLS, BS, TOK), bf16),
            pltpu.VMEM((COLS, KB * BS, TOK), bf16),
            pltpu.VMEM((COLS, 2 * BS, TOK), bf16),
            pltpu.VMEM((NX * NZ * CAP, 2 * BS, BS), bf16),
            pltpu.SemaphoreType.DMA((16,)),
            pltpu.SemaphoreType.DMA((3 * COLS,)),
            pltpu.SemaphoreType.DMA((6,)),
        ],
        flops=8 * BLOCKS * BS * BS * TOK, bytes_accessed=14 * 2**20, vmem_mib=VMEM_MIB,
    )(a, ac, b, bc, gate_t, up_t, hidden, block_rows, place)

    def over_x(parts):
        parts = [parts[0]] + [shift(parts[i], "x", i) for i in (1, 3, 2)]
        return sum(part.astype(f32) for part in parts)

    def halve(keep, axis):
        half = keep.shape[0] // 2
        return keep[:half] + swap(keep[half:].astype(bf16), axis).astype(f32)

    got = swap(send.reshape(-1, BS), "z2").reshape(NX, -1, BS)
    keep = keep.reshape(NX, -1, BS)
    first = over_x([part.reshape(-1, BS) for part in firsts])
    second = over_x([(keep[i].astype(f32) + got[i].astype(f32)).astype(bf16) for i in range(NX)])
    first = halve(halve(halve(first, "z2"), "z4"), "z8")
    second = halve(halve(second, "z4"), "z8")
    return jnp.concatenate([first, second], 0).reshape(1, 1, CAP, 2, BS, BS)


def solution(mesh):
    fine = Mesh(mesh.devices.reshape(tuple(AXES.values())), tuple(AXES))
    dp, tensor = ("z8", "z4", "z2", "x"), ("y", "zh", "core")
    in_specs = (
        P(dp, tensor),
        P(dp, tensor),
        P(tensor, None, None, None),
        P(tensor, None, None, None),
        P(tensor, None),
        P(tensor, None),
    )
    out_specs = P(tensor, dp, None, None, None, None)
    return jax.shard_map(body, mesh=fine, in_specs=in_specs, out_specs=out_specs, check_vma=False)
```

```python
import functools

import jax
import jax.numpy as jnp
from jax import lax
from jax.experimental import pallas as pl
from jax.experimental.pallas import tpu as pltpu
from jax.sharding import Mesh, PartitionSpec as P

BS = 128
KB = 8
COLS = 7
BLOCKS = COLS * KB
TOK = 512
ROWS = 32
NX, NZ, CAP = 4, 8, 2
VMEM_MIB = 45
AXES = {"z8": 2, "z4": 2, "z2": 2, "x": 4, "y": 4, "zh": 2, "core": 2}
VMEM = pl.BlockSpec(memory_space=pltpu.VMEM)
HBM = pl.BlockSpec(memory_space=pltpu.HBM)
ANY = pl.BlockSpec(memory_space=pl.ANY)
SMEM = pl.BlockSpec(memory_space=pltpu.SMEM)


def swap(value, axis):
    return lax.ppermute(value, axis, [(0, 1), (1, 0)])


def shift(value, axis, step):
    size = AXES[axis]
    return lax.ppermute(value, axis, [(i, (i + step) % size) for i in range(size)])


def spread(value, axis):
    return lax.all_to_all(jnp.broadcast_to(value[None], (AXES[axis],) + value.shape), axis, 0, 0, tiled=True)


def call(kernel, out_shape, in_specs, out_specs, scratch=(), flops=0, bytes_accessed=0, vmem_mib=16):
    return pl.pallas_call(
        kernel,
        out_shape=out_shape,
        in_specs=in_specs,
        out_specs=out_specs,
        scratch_shapes=list(scratch),
        compiler_params=pltpu.CompilerParams(vmem_limit_bytes=vmem_mib * 2**20),
        cost_estimate=pl.CostEstimate(flops=flops, bytes_accessed=bytes_accessed, transcendentals=0),
    )


def place_kernel(owner_ref, gate_ref, up_ref, hidden_ref, near_ref, place_ref, seen_ref):
    my_x = lax.axis_index("x")
    my_z = lax.axis_index("z8") * 4 + lax.axis_index("z4") * 2 + lax.axis_index("z2")

    def clear(i, carry):
        seen_ref[i] = jnp.int32(0)
        return carry

    lax.fori_loop(0, NX * NZ, clear, 0)

    def place(i, carry):
        owner = owner_ref[i // KB, i % KB]
        slot = seen_ref[owner]
        seen_ref[owner] = slot + 1
        x = (owner % NX - my_x + NX) % NX
        z = (owner // NX) ^ my_z
        other = z & 1
        rest = (z & 2) + (z >> 2)
        first = x * NZ + other * 4 + rest
        second = NX * NZ + (1 - other) * (NX * 4) + x * 4 + rest
        place_ref[i] = jnp.where(slot == 0, first, second)
        return carry

    lax.fori_loop(0, BLOCKS, place, 0)


def block_kernel(
    a_ref, ac_ref, b_ref, bc_ref, gate_ref, up_ref, hidden_ref, rows_ref, place_ref,
    send_ref, first0_ref, first1_ref, first2_ref, first3_ref, keep_ref, x_ref, w_ref, h_ref, picked_ref, act_ref, out_ref, x_sem, w_sem, out_sem,
):
    zh = lax.axis_index("zh")
    core = lax.axis_index("core")
    x_copies = []
    for i, (ref, z, c) in enumerate(
        ((a_ref, zh, core), (ac_ref, zh, 1 - core), (b_ref, 1 - zh, core), (bc_ref, 1 - zh, 1 - core))
    ):
        for y in range(4):
            at = (y * 4 + z * 2 + c) * 2
            x_copies.append(pltpu.make_async_copy(ref.at[y], x_ref.at[pl.ds(at, 2)], x_sem.at[i * 4 + y]))
    w_copies = []
    for c in range(COLS):
        w_copies.append((
            pltpu.make_async_copy(gate_ref.at[c], w_ref.at[c, pl.ds(0, BS)], w_sem.at[3 * c]),
            pltpu.make_async_copy(up_ref.at[c], w_ref.at[c, pl.ds(BS, BS)], w_sem.at[3 * c + 1]),
            pltpu.make_async_copy(hidden_ref.at[c], h_ref.at[c], w_sem.at[3 * c + 2]),
        ))
    for copy in x_copies:
        copy.start()
    for copies in w_copies:
        for copy in copies:
            copy.start()
    out_ref[...] = jnp.zeros_like(out_ref)
    for copy in x_copies:
        copy.wait()
    for c in range(COLS):
        now_ref = picked_ref.at[c]
        for k in range(KB):
            now_ref[k * BS:(k + 1) * BS] = x_ref[rows_ref[c, k]]
        for copy in w_copies[c]:
            copy.wait()
        pre = jnp.dot(w_ref[c], now_ref[...], preferred_element_type=jnp.float32)
        gate, up = pre[:BS], pre[BS:]
        s = jax.nn.sigmoid(gate)
        h = h_ref[c].astype(jnp.float32)
        act_ref[c, :BS] = (h * up * (s * (1.0 + gate * (1.0 - s)))).astype(jnp.bfloat16)
        act_ref[c, BS:] = (h * (gate * s)).astype(jnp.bfloat16)
    for c in range(COLS):
        value = lax.dot_general(
            picked_ref[c], act_ref[c], (((1,), (1,)), ((), ())), preferred_element_type=jnp.float32
        ).astype(jnp.bfloat16)
        for k in range(KB):
            for m in range(2):
                out_ref[place_ref[c * KB + k], m * BS:(m + 1) * BS] = value[k * BS:(k + 1) * BS, m * BS:(m + 1) * BS]
    places = [NX * NZ] + [i * NZ for i in range(NX)] + [NX * NZ + NX * 4]
    out_copies = []
    for i, ref in enumerate((send_ref, first0_ref, first1_ref, first2_ref, first3_ref, keep_ref)):
        out_copies.append(pltpu.make_async_copy(out_ref.at[pl.ds(places[i], ref.shape[0])], ref, out_sem.at[i]))
    for copy in out_copies:
        copy.start()
    for copy in out_copies:
        copy.wait()


def body(x_panel, grad_hidden, gate_blocks, up_blocks, block_rows, block_owner):
    bf16, f32 = jnp.bfloat16, jnp.float32
    own = x_panel.T.reshape(2, BS, TOK)
    far = swap(own, "zh")
    a = spread(own, "y")
    gate_t, up_t = (w.transpose(0, 3, 1, 2).reshape(COLS, BS, KB * BS) for w in (gate_blocks, up_blocks))
    hidden = grad_hidden.T.reshape(COLS, BS, TOK)
    corners = [v[0, :8] for v in (gate_t, up_t, hidden, a[0])]
    place = call(
        place_kernel, jax.ShapeDtypeStruct((BLOCKS,), jnp.int32), [SMEM] + [ANY] * 4, SMEM,
        [pltpu.SMEM((NX * NZ,), jnp.int32)],
    )(block_owner, *corners)
    ac = swap(a, "core")
    far, place = lax.optimization_barrier((far, place))
    b = spread(far, "y")
    bc = swap(b, "core")

    counts = (NX * 4, NZ, NZ, NZ, NZ, NX * 4)
    send, *firsts, keep = call(
        block_kernel, [jax.ShapeDtypeStruct((count, 2 * BS, BS), bf16) for count in counts],
        [HBM] * 7 + [SMEM, SMEM], [ANY] * 6,
        [
            pltpu.VMEM((ROWS, BS, TOK), bf16),
            pltpu.VMEM((COLS, 2 * BS, KB * BS), bf16),
            pltpu.VMEM((COLS, BS, TOK), bf16),
            pltpu.VMEM((COLS, KB * BS, TOK), bf16),
            pltpu.VMEM((COLS, 2 * BS, TOK), bf16),
            pltpu.VMEM((NX * NZ * CAP, 2 * BS, BS), bf16),
            pltpu.SemaphoreType.DMA((16,)),
            pltpu.SemaphoreType.DMA((3 * COLS,)),
            pltpu.SemaphoreType.DMA((6,)),
        ],
        flops=8 * BLOCKS * BS * BS * TOK, bytes_accessed=14 * 2**20, vmem_mib=VMEM_MIB,
    )(a, ac, b, bc, gate_t, up_t, hidden, block_rows, place)

    def over_x(parts):
        parts = [parts[0]] + [shift(parts[i], "x", i) for i in (1, 3, 2)]
        return sum(part.astype(f32) for part in parts)

    def halve(keep, axis):
        half = keep.shape[0] // 2
        return keep[:half] + swap(keep[half:].astype(bf16), axis).astype(f32)

    got = swap(send.reshape(-1, BS), "z2").reshape(NX, -1, BS)
    keep = keep.reshape(NX, -1, BS)
    first = over_x([part.reshape(-1, BS) for part in firsts])
    second = over_x([(keep[i].astype(f32) + got[i].astype(f32)).astype(bf16) for i in range(NX)])
    first = halve(halve(halve(first, "z2"), "z4"), "z8")
    second = halve(halve(second, "z4"), "z8")
    return jnp.concatenate([first, second], 0).reshape(1, 1, CAP, 2, BS, BS)


def solution(mesh):
    fine = Mesh(mesh.devices.reshape(tuple(AXES.values())), tuple(AXES))
    dp, tensor = ("z8", "z4", "z2", "x"), ("y", "zh", "core")
    in_specs = (
        P(dp, tensor),
        P(dp, tensor),
        P(tensor, None, None, None),
        P(tensor, None, None, None),
        P(tensor, None),
        P(tensor, None),
    )
    out_specs = P(tensor, dp, None, None, None, None)
    return jax.shard_map(body, mesh=fine, in_specs=in_specs, out_specs=out_specs, check_vma=False)
```

```python
import functools

import jax
import jax.numpy as jnp
from jax import lax
from jax.experimental import pallas as pl
from jax.experimental.pallas import tpu as pltpu
from jax.sharding import Mesh, PartitionSpec as P

BS = 128
KB = 8
COLS = 7
BLOCKS = COLS * KB
TOK = 512
ROWS = 32
NX, NZ, CAP = 4, 8, 2
VMEM_MIB = 45
AXES = {"z8": 2, "z4": 2, "z2": 2, "x": 4, "y": 4, "zh": 2, "core": 2}
VMEM = pl.BlockSpec(memory_space=pltpu.VMEM)
HBM = pl.BlockSpec(memory_space=pltpu.HBM)
ANY = pl.BlockSpec(memory_space=pl.ANY)
SMEM = pl.BlockSpec(memory_space=pltpu.SMEM)


def swap(value, axis):
    return lax.ppermute(value, axis, [(0, 1), (1, 0)])


def shift(value, axis, step):
    size = AXES[axis]
    return lax.ppermute(value, axis, [(i, (i + step) % size) for i in range(size)])


def spread(value, axis):
    return lax.all_to_all(jnp.broadcast_to(value[None], (AXES[axis],) + value.shape), axis, 0, 0, tiled=True)


def call(kernel, out_shape, in_specs, out_specs, scratch=(), flops=0, bytes_accessed=0, vmem_mib=16):
    return pl.pallas_call(
        kernel,
        out_shape=out_shape,
        in_specs=in_specs,
        out_specs=out_specs,
        scratch_shapes=list(scratch),
        compiler_params=pltpu.CompilerParams(vmem_limit_bytes=vmem_mib * 2**20),
        cost_estimate=pl.CostEstimate(flops=flops, bytes_accessed=bytes_accessed, transcendentals=0),
    )


def place_kernel(owner_ref, gate_ref, up_ref, hidden_ref, near_ref, place_ref, seen_ref):
    my_x = lax.axis_index("x")
    my_z = lax.axis_index("z8") * 4 + lax.axis_index("z4") * 2 + lax.axis_index("z2")

    def clear(i, carry):
        seen_ref[i] = jnp.int32(0)
        return carry

    lax.fori_loop(0, NX * NZ, clear, 0)

    def place(i, carry):
        owner = owner_ref[i // KB, i % KB]
        slot = seen_ref[owner]
        seen_ref[owner] = slot + 1
        x = (owner % NX - my_x + NX) % NX
        z = (owner // NX) ^ my_z
        other = z & 1
        rest = (z & 2) + (z >> 2)
        first = x * NZ + other * 4 + rest
        second = NX * NZ + (1 - other) * (NX * 4) + x * 4 + rest
        place_ref[i] = jnp.where(slot == 0, first, second)
        return carry

    lax.fori_loop(0, BLOCKS, place, 0)


def block_kernel(
    a_ref, ac_ref, b_ref, bc_ref, gate_ref, up_ref, hidden_ref, rows_ref, place_ref,
    send_ref, first0_ref, first1_ref, first2_ref, first3_ref, keep_ref, x_ref, w_ref, h_ref, picked_ref, act_ref, out_ref, x_sem, w_sem, out_sem,
):
    zh = lax.axis_index("zh")
    core = lax.axis_index("core")
    x_copies = []
    for i, (ref, z, c) in enumerate(
        ((a_ref, zh, core), (ac_ref, zh, 1 - core), (b_ref, 1 - zh, core), (bc_ref, 1 - zh, 1 - core))
    ):
        for y in range(4):
            at = (y * 4 + z * 2 + c) * 2
            x_copies.append(pltpu.make_async_copy(ref.at[y], x_ref.at[pl.ds(at, 2)], x_sem.at[i * 4 + y]))
    w_copies = []
    for c in range(COLS):
        w_copies.append((
            pltpu.make_async_copy(gate_ref.at[c], w_ref.at[c, pl.ds(0, BS)], w_sem.at[3 * c]),
            pltpu.make_async_copy(up_ref.at[c], w_ref.at[c, pl.ds(BS, BS)], w_sem.at[3 * c + 1]),
            pltpu.make_async_copy(hidden_ref.at[c], h_ref.at[c], w_sem.at[3 * c + 2]),
        ))
    for copy in x_copies:
        copy.start()
    for copies in w_copies:
        for copy in copies:
            copy.start()
    out_ref[...] = jnp.zeros_like(out_ref)
    for copy in x_copies:
        copy.wait()
    for c in range(COLS):
        now_ref = picked_ref.at[c]
        for k in range(KB):
            now_ref[k * BS:(k + 1) * BS] = x_ref[rows_ref[c, k]]
        for copy in w_copies[c]:
            copy.wait()
        pre = jnp.dot(w_ref[c], now_ref[...], preferred_element_type=jnp.float32)
        gate, up = pre[:BS], pre[BS:]
        s = jax.nn.sigmoid(gate)
        h = h_ref[c].astype(jnp.float32)
        act_ref[c, :BS] = (h * up * (s * (1.0 + gate * (1.0 - s)))).astype(jnp.bfloat16)
        act_ref[c, BS:] = (h * (gate * s)).astype(jnp.bfloat16)
    for c in range(COLS):
        value = lax.dot_general(
            picked_ref[c], act_ref[c], (((1,), (1,)), ((), ())), preferred_element_type=jnp.float32
        ).astype(jnp.bfloat16)
        for k in range(KB):
            for m in range(2):
                out_ref[place_ref[c * KB + k], m * BS:(m + 1) * BS] = value[k * BS:(k + 1) * BS, m * BS:(m + 1) * BS]
    places = [NX * NZ] + [i * NZ for i in range(NX)] + [NX * NZ + NX * 4]
    out_copies = []
    for i, ref in enumerate((send_ref, first0_ref, first1_ref, first2_ref, first3_ref, keep_ref)):
        out_copies.append(pltpu.make_async_copy(out_ref.at[pl.ds(places[i], ref.shape[0])], ref, out_sem.at[i]))
    for copy in out_copies:
        copy.start()
    for copy in out_copies:
        copy.wait()


def body(x_panel, grad_hidden, gate_blocks, up_blocks, block_rows, block_owner):
    bf16, f32 = jnp.bfloat16, jnp.float32
    own = x_panel.T.reshape(2, BS, TOK)
    far = swap(own, "zh")
    a = spread(own, "y")
    gate_t, up_t = (w.transpose(0, 3, 1, 2).reshape(COLS, BS, KB * BS) for w in (gate_blocks, up_blocks))
    hidden = grad_hidden.T.reshape(COLS, BS, TOK)
    corners = [v[0, :8] for v in (gate_t, up_t, hidden, a[0])]
    place = call(
        place_kernel, jax.ShapeDtypeStruct((BLOCKS,), jnp.int32), [SMEM] + [ANY] * 4, SMEM,
        [pltpu.SMEM((NX * NZ,), jnp.int32)],
    )(block_owner, *corners)
    ac = swap(a, "core")
    far, place = lax.optimization_barrier((far, place))
    b = spread(far, "y")
    bc = swap(b, "core")

    counts = (NX * 4, NZ, NZ, NZ, NZ, NX * 4)
    send, *firsts, keep = call(
        block_kernel, [jax.ShapeDtypeStruct((count, 2 * BS, BS), bf16) for count in counts],
        [HBM] * 7 + [SMEM, SMEM], [ANY] * 6,
        [
            pltpu.VMEM((ROWS, BS, TOK), bf16),
            pltpu.VMEM((COLS, 2 * BS, KB * BS), bf16),
            pltpu.VMEM((COLS, BS, TOK), bf16),
            pltpu.VMEM((COLS, KB * BS, TOK), bf16),
            pltpu.VMEM((COLS, 2 * BS, TOK), bf16),
            pltpu.VMEM((NX * NZ * CAP, 2 * BS, BS), bf16),
            pltpu.SemaphoreType.DMA((16,)),
            pltpu.SemaphoreType.DMA((3 * COLS,)),
            pltpu.SemaphoreType.DMA((6,)),
        ],
        flops=8 * BLOCKS * BS * BS * TOK, bytes_accessed=14 * 2**20, vmem_mib=VMEM_MIB,
    )(a, ac, b, bc, gate_t, up_t, hidden, block_rows, place)

    def over_x(parts):
        parts = [parts[0]] + [shift(parts[i], "x", i) for i in (1, 3, 2)]
        return sum(part.astype(f32) for part in parts)

    def halve(keep, axis):
        half = keep.shape[0] // 2
        return keep[:half] + swap(keep[half:].astype(bf16), axis).astype(f32)

    got = swap(send.reshape(-1, BS), "z2").reshape(NX, -1, BS)
    keep = keep.reshape(NX, -1, BS)
    first = over_x([part.reshape(-1, BS) for part in firsts])
    second = over_x([(keep[i].astype(f32) + got[i].astype(f32)).astype(bf16) for i in range(NX)])
    first = halve(halve(first, "z2"), "z4")
    second = halve(second, "z4")
    half = first.shape[0] // 2
    got = swap(jnp.concatenate([first[half:], second[half:]], 0).astype(bf16), "z8")
    return (jnp.concatenate([first[:half], second[:half]], 0) + got.astype(f32)).reshape(1, 1, CAP, 2, BS, BS)


def solution(mesh):
    fine = Mesh(mesh.devices.reshape(tuple(AXES.values())), tuple(AXES))
    dp, tensor = ("z8", "z4", "z2", "x"), ("y", "zh", "core")
    in_specs = (
        P(dp, tensor),
        P(dp, tensor),
        P(tensor, None, None, None),
        P(tensor, None, None, None),
        P(tensor, None),
        P(tensor, None),
    )
    out_specs = P(tensor, dp, None, None, None, None)
    return jax.shard_map(body, mesh=fine, in_specs=in_specs, out_specs=out_specs, check_vma=False)
```
